32 devices in a mesh: dp: 16 (over z, y, x), tensor: 2 (over core).
Axes of the slice: x: 2, y: 2, z: 4, core: 2. Of those that a mesh axis runs over, the one named last changes fastest.
Arguments:
- hidden_in: bfloat16 [4096, 768], P('dp'), may hold values from -6 to 6
- lengths: int32 [16], P('dp'), may hold values from 128 to 256, as said below
- neighbours: bfloat16 [128, 128, 768], P('dp'), may hold values from -6 to 6
- assign: int32 [64, 2], P('dp'), may hold values from 0 to 7
- cotangent: bfloat16 [4096, 768], P('dp'), may hold values from -6 to 6
- norm_gain: float32 [5, 768], replicated, may hold values from 0.5 to 1.5
- norm_bias: float32 [5, 768], replicated, may hold values from -1.75 to 1.75
- sa_qkv: bfloat16 [2, 3, 768, 768], P(None, None, None, 'tensor'), may hold values from -0.21875 to 0.21875
- sa_bias: float32 [2, 2, 768], P(None, None, 'tensor'), may hold values from -1.75 to 1.75
- sa_out: bfloat16 [2, 768, 768], P(None, 'tensor'), may hold values from -0.875 to 0.875
- sa_out_bias: float32 [2, 768], replicated, may hold values from -1.75 to 1.75
- ca_qkv: bfloat16 [3, 768, 768], P(None, None, 'tensor'), may hold values from -0.21875 to 0.21875
- ca_bias: float32 [2, 768], P(None, 'tensor'), may hold values from -1.75 to 1.75
- ca_out: bfloat16 [768, 768], P('tensor'), may hold values from -0.875 to 0.875
- ca_out_bias: float32 [768], replicated, may hold values from -1.75 to 1.75
- mlp_in: bfloat16 [2, 768, 3072], P(None, None, 'tensor'), may hold values from -0.21875 to 0.21875
- mlp_in_bias: float32 [2, 3072], P(None, 'tensor'), may hold values from -1.75 to 1.75
- mlp_out: bfloat16 [2, 3072, 768], P(None, 'tensor'), may hold values from -0.109375 to 0.109375
- mlp_out_bias: float32 [2, 768], replicated, may hold values from -1.75 to 1.75
Outputs:
- hidden_out: bfloat16 [4096, 768], P('dp')
- input_grad: float32 [4096, 768], P('dp')
- neighbour_grad: float32 [128, 128, 768], P('dp', None, 'tensor')
- norm_gain_grad: float32 [5, 768], replicated
- norm_bias_grad: float32 [5, 768], replicated
- sa_qkv_grad: float32 [2, 3, 768, 768], P(None, None, 'dp', 'tensor')
- sa_bias_grad: float32 [2, 2, 768], P(None, None, 'tensor')
- sa_out_grad: float32 [2, 768, 768], P(None, 'tensor', 'dp')
- sa_out_bias_grad: float32 [2, 768], replicated
- ca_qkv_grad: float32 [3, 768, 768], P(None, 'dp', 'tensor')
- ca_bias_grad: float32 [2, 768], P(None, 'tensor')
- ca_out_grad: float32 [768, 768], P('tensor', 'dp')
- ca_out_bias_grad: float32 [768], replicated
- mlp_in_grad: float32 [2, 768, 3072], P(None, 'dp', 'tensor')
- mlp_in_bias_grad: float32 [2, 3072], P(None, 'tensor')
- mlp_out_grad: float32 [2, 3072, 768], P(None, 'tensor', 'dp')
- mlp_out_bias_grad: float32 [2, 768], replicated
The draws below stay inside these ranges and needn't reach their ends.
Inputs may be any that keep to these rules, and one draw needn't show every extreme that they name: `lengths`: live tokens of each bucket, counted from its start, the rest padding; in every draw some bucket is full (256). `assign`: which of its bucket's 8 encoded neighbours each span reads, for each of its 2 slots.
All inputs are finite; a program needn't handle non-finite values.
Results may differ from the reference program's by a relative error of at most 0.03.
Values may be sent and summed in bfloat16 or wider, within the bound.
A program may use at most 192 MiB of HBM per device.

```python
import jax
import jax.numpy as jnp
from jax import lax

D = 768
HEADS = 12
HEAD_DIM = 64
FF = 3072
SEQ = 256
SPAN = 64
NBR_LEN = 128
NEIGH = 2
SPANS = 4
POOL = 8
BUCKETS = 16
TOKENS = 4096
N_TENSOR = 2


def draw_lengths(key, part):
    key = jax.random.fold_in(key, 11)
    first_key, second_key = jax.random.split(key)
    drawn = jax.random.randint(first_key, (BUCKETS,), SEQ // 2, SEQ + 1)
    full_one = jax.random.randint(second_key, (), 0, BUCKETS)
    return jnp.where(jnp.arange(BUCKETS) == full_one, SEQ, drawn).astype(jnp.int32)


def with_ends(array, key, least, largest):
    index_at = [jax.random.randint(jax.random.fold_in(key, axis), (), 0, length) for axis, length in enumerate(array.shape)]
    main_axis = array.shape.index(max(array.shape))
    next_to = index_at[:main_axis] + [(index_at[main_axis] + 1) % array.shape[main_axis]] + index_at[main_axis + 1:]
    return array.at[tuple(index_at)].set(least).at[tuple(next_to)].set(largest)


def spiked(entries, own_key, source, target, blocks, factor):
    def block_of(dim):
        return (jnp.arange(entries.shape[dim]) // (entries.shape[dim] // blocks)).reshape((-1,) + (1,) * (entries.ndim - 1 - dim))

    one_side = jax.random.permutation(own_key, blocks)[block_of(target)]
    far = (block_of(target) + blocks // 2) % blocks
    return jnp.where((block_of(source) == one_side) | (block_of(source) == far), factor * entries, entries)


def shard_levels(own_key, extent, cuts, smallest, top_value):
    loudness, own = 1.0, jax.random.fold_in(own_key, 6)
    for dim, shards_of in cuts:
        heights = jnp.exp(jax.random.uniform(jax.random.fold_in(own, dim), (shards_of,), jnp.float32, smallest / len(cuts), top_value / len(cuts)))
        loudness = loudness * jnp.repeat(heights, extent[dim] // shards_of).reshape([-1 if axis == dim else 1 for axis in range(len(extent))])
    return loudness


def noise(stream_key, shape, scale, most, shards=(), kind=jnp.bfloat16):
    values = scale * jax.random.normal(stream_key, shape, jnp.float32)
    if shards:
        values = values * shard_levels(stream_key, shape, shards, -0.22, 0.18)
    return jnp.clip(values, -most, most).astype(kind)


def noise_with(own_key, extent, spread, most, cuts, heavy, kind=jnp.bfloat16):
    result = spread * jax.random.normal(own_key, extent, jnp.float32)
    if cuts:
        result = result * shard_levels(own_key, extent, cuts, -0.22, 0.18)
    return jnp.clip(spiked(result, jax.random.fold_in(own_key, 3), *heavy), -most, most).astype(kind)


def setup_inputs(seed: int = 0) -> dict:
    arg_keys = jax.random.split(jax.random.key(seed), 20)
    hidden_in = noise(arg_keys[0], (TOKENS, D), 1.0, 6.0, ((0, 16),))
    lengths = draw_lengths(jax.random.fold_in(arg_keys[19], 71), 0)
    neighbours = noise(arg_keys[2], (BUCKETS * POOL, NBR_LEN, D), 1.0, 6.0, ((0, 16),))
    assign = with_ends(jax.random.randint(arg_keys[3], (BUCKETS * SPANS, NEIGH), 0, POOL), jax.random.fold_in(arg_keys[3], 1), 0, POOL - 1).astype(jnp.int32)
    cotangent = noise_with(arg_keys[4], (TOKENS, D), 1.0, 6.0, ((0, 16),), (0, 1, 16, 2.0))
    norm_gain = jnp.clip(1.0 + 0.1 * jax.random.normal(arg_keys[5], (5, D), jnp.float32), 0.5, 1.5)
    norm_bias = noise(arg_keys[6], (5, D), 0.3, 1.75, (), jnp.float32)
    sa_qkv = noise(arg_keys[7], (2, 3, D, D), D ** -0.5, 0.21875, ((3, 2),))
    sa_bias = noise(arg_keys[8], (2, 2, D), 0.3, 1.75, ((2, 2),), jnp.float32)
    sa_out = noise(arg_keys[9], (2, D, D), (D // 16) ** -0.5, 0.875, ((1, 2),))
    sa_out_bias = noise(arg_keys[10], (2, D), 0.3, 1.75, (), jnp.float32)
    ca_qkv = noise(arg_keys[11], (3, D, D), D ** -0.5, 0.21875, ((2, 2),))
    ca_bias = noise(arg_keys[12], (2, D), 0.3, 1.75, ((1, 2),), jnp.float32)
    ca_out = noise(arg_keys[13], (D, D), (D // 16) ** -0.5, 0.875, ((0, 2),))
    ca_out_bias = noise(arg_keys[14], (D,), 0.3, 1.75, (), jnp.float32)
    mlp_in = noise(arg_keys[15], (2, D, FF), D ** -0.5, 0.21875, ((2, 2),))
    mlp_in_bias = noise(arg_keys[16], (2, FF), 0.3, 1.75, ((1, 2),), jnp.float32)
    mlp_out = noise(arg_keys[17], (2, FF, D), FF ** -0.5, 0.109375, ((1, 2),))
    mlp_out_bias = noise(arg_keys[18], (2, D), 0.3, 1.75, (), jnp.float32)
    return {"hidden_in": hidden_in, "lengths": lengths, "neighbours": neighbours, "assign": assign, "cotangent": cotangent, "norm_gain": norm_gain, "norm_bias": norm_bias, "sa_qkv": sa_qkv, "sa_bias": sa_bias, "sa_out": sa_out, "sa_out_bias": sa_out_bias, "ca_qkv": ca_qkv, "ca_bias": ca_bias, "ca_out": ca_out, "ca_out_bias": ca_out_bias, "mlp_in": mlp_in, "mlp_in_bias": mlp_in_bias, "mlp_out": mlp_out, "mlp_out_bias": mlp_out_bias}


HIGH = lax.Precision.HIGHEST
EPSILON = 1e-05
SCORE_SCALE = 0.125
MASKED = -1e+30

@jax.custom_vjp
def low(v):
    return lax.optimization_barrier(v.astype(jnp.bfloat16)).astype(jnp.float32)

@jax.custom_vjp
def low_back(v):
    return v

def low_keep(v):
    return (low(v), None)

def low_pass(kept, grad):
    return (grad,)

def back_keep(v):
    return (v, None)

def back_low(kept, grad):
    return (low(grad),)
low.defvjp(low_keep, low_pass)
low_back.defvjp(back_keep, back_low)

def round_both(values):
    return low(low_back(values))

def layer_norm(hidden, gain_vec, shift_vec):
    centre = lax.optimization_barrier(jnp.mean(hidden, axis=-1, keepdims=True))
    centred = hidden - centre
    variance = lax.optimization_barrier(jnp.mean(centred * centred, axis=-1, keepdims=True))
    return centred * lax.rsqrt(variance + EPSILON) * gain_vec + shift_vec

def project(left, weight):
    return jnp.dot(left, weight, precision=HIGH)

def branch_out(values, weight, bias_vec):
    row_count = values.shape[0]
    parts = jnp.einsum('sgd,gde->gse', values.reshape(row_count, N_TENSOR, -1), weight.reshape(N_TENSOR, -1, weight.shape[1]), precision=HIGH)
    return low_back(lax.optimization_barrier(jnp.sum(low(parts), axis=0)) + bias_vec)

def causal_attention(queries, key_heads, value_heads):
    row_count = queries.shape[0]
    block_rows = min(512, row_count)
    block_count = row_count // block_rows

    @jax.checkpoint
    def one_block(inputs):
        query_block, first_row = inputs
        scores = low_back(SCORE_SCALE * jnp.einsum('qhd,khd->hqk', query_block, key_heads, precision=HIGH))
        row_ids = first_row + jnp.arange(block_rows, dtype=jnp.int32)
        col_ids = jnp.arange(row_count, dtype=jnp.int32)
        scores = jnp.where((col_ids[None, :] <= row_ids[:, None])[None], scores, MASKED)
        weights = low(jax.nn.softmax(scores, axis=-1))
        return jnp.einsum('hqk,khd->qhd', weights, value_heads, precision=HIGH)
    starts = jnp.arange(block_count, dtype=jnp.int32) * block_rows
    mixed = lax.map(one_block, (queries.reshape((block_count, block_rows) + queries.shape[1:]), starts))
    return mixed.reshape(queries.shape)

def self_block(hidden, gain_vec, shift_vec, qkv_weight, qkv_bias, out_weight, out_bias):
    row_count = hidden.shape[0]
    normed = low(layer_norm(hidden, gain_vec, shift_vec))
    queries = round_both(project(normed, qkv_weight[0]) + qkv_bias[0]).reshape(row_count, HEADS, HEAD_DIM)
    key_heads = round_both(project(normed, qkv_weight[1])).reshape(row_count, HEADS, HEAD_DIM)
    value_heads = round_both(project(normed, qkv_weight[2]) + qkv_bias[1]).reshape(row_count, HEADS, HEAD_DIM)
    attended = round_both(causal_attention(queries, key_heads, value_heads).reshape(row_count, D))
    return hidden + branch_out(attended, out_weight, out_bias)

def shift_up(values):
    offset_rows = SPAN - 1
    return jnp.concatenate([values[offset_rows:], jnp.zeros((offset_rows,) + values.shape[1:], values.dtype)], axis=0)

def shift_down(values):
    offset_rows = SPAN - 1
    return jnp.concatenate([jnp.zeros((offset_rows,) + values.shape[1:], values.dtype), values[:values.shape[0] - offset_rows]], axis=0)

def cross_block(hidden, gain_vec, shift_vec, pool_rows, assign_rows, qkv_weight, qkv_bias, out_weight, out_bias):
    row_count = hidden.shape[0]
    normed = low(layer_norm(hidden, gain_vec, shift_vec))
    flat_pool = pool_rows.reshape(-1, D)
    queries = round_both(project(normed, qkv_weight[0]) + qkv_bias[0])
    pool_keys = round_both(project(flat_pool, qkv_weight[1])).reshape(POOL, NBR_LEN, HEADS, HEAD_DIM)
    pool_values = round_both(project(flat_pool, qkv_weight[2]) + qkv_bias[1]).reshape(POOL, NBR_LEN, HEADS, HEAD_DIM)
    span_queries = shift_up(queries).reshape(SPANS, SPAN, HEADS, HEAD_DIM)
    span_keys = pool_keys[assign_rows].reshape(SPANS, NEIGH * NBR_LEN, HEADS, HEAD_DIM)
    span_values = pool_values[assign_rows].reshape(SPANS, NEIGH * NBR_LEN, HEADS, HEAD_DIM)
    scores = low_back(SCORE_SCALE * jnp.einsum('cqhd,ckhd->chqk', span_queries, span_keys, precision=HIGH))
    weights = low(jax.nn.softmax(scores, axis=-1))
    mixed = jnp.einsum('chqk,ckhd->cqhd', weights, span_values, precision=HIGH).reshape(row_count, D)
    attended = round_both(shift_down(mixed))
    return hidden + branch_out(attended, out_weight, out_bias)

def ffn_block(hidden, gain_vec, shift_vec, in_weight, in_bias, out_weight, out_bias):
    normed = low(layer_norm(hidden, gain_vec, shift_vec))
    pre_act = low_back(project(normed, in_weight) + in_bias)
    activated = low(jax.nn.gelu(pre_act, approximate=False))
    return hidden + branch_out(activated, out_weight, out_bias)

def layers(weights, inputs, pool_rows, assign_rows, live):
    gains, shifts, sa_qkv, sa_bias, sa_out, sa_out_bias, ca_qkv, ca_bias, ca_out, ca_out_bias, mlp_in, mlp_in_bias, mlp_out, mlp_out_bias = weights
    hidden = self_block(inputs, gains[0], shifts[0], sa_qkv[0], sa_bias[0], sa_out[0], sa_out_bias[0])
    hidden = cross_block(hidden, gains[1], shifts[1], pool_rows, assign_rows, ca_qkv, ca_bias, ca_out, ca_out_bias)
    hidden = ffn_block(hidden, gains[2], shifts[2], mlp_in[0], mlp_in_bias[0], mlp_out[0], mlp_out_bias[0])
    hidden = self_block(hidden, gains[3], shifts[3], sa_qkv[1], sa_bias[1], sa_out[1], sa_out_bias[1])
    hidden = ffn_block(hidden, gains[4], shifts[4], mlp_in[1], mlp_in_bias[1], mlp_out[1], mlp_out_bias[1])
    return live * hidden

def reference(hidden_in, lengths, neighbours, assign, cotangent, norm_gain, norm_bias, sa_qkv, sa_bias, sa_out, sa_out_bias, ca_qkv, ca_bias, ca_out, ca_out_bias, mlp_in, mlp_in_bias, mlp_out, mlp_out_bias):
    params = tuple((item.astype(jnp.float32) for item in (norm_gain, norm_bias, sa_qkv, sa_bias, sa_out, sa_out_bias, ca_qkv, ca_bias, ca_out, ca_out_bias, mlp_in, mlp_in_bias, mlp_out, mlp_out_bias)))
    inputs_all = hidden_in.astype(jnp.float32).reshape(BUCKETS, SEQ, D)
    pool_all = neighbours.astype(jnp.float32).reshape(BUCKETS, POOL, NBR_LEN, D)
    assign_all = assign.reshape(BUCKETS, SPANS, NEIGH)
    cotangent_all = cotangent.astype(jnp.float32).reshape(BUCKETS, SEQ, D)

    def one_bucket(totals, item):
        bucket_in, bucket_pool, bucket_assign, bucket_len, bucket_cot = item
        live = (jnp.arange(SEQ, dtype=jnp.int32) < bucket_len).astype(jnp.float32)[:, None]

        def forward(weights, inputs, pool_rows):
            return layers(weights, inputs, pool_rows, bucket_assign, live)
        bucket_out, backward = jax.vjp(forward, params, bucket_in, bucket_pool)
        weight_grads, bucket_in_grad, bucket_pool_grad = backward(bucket_cot)
        totals = jax.tree.map(lambda left, right: left + right, totals, weight_grads)
        return (totals, (bucket_out, bucket_in_grad, bucket_pool_grad))
    zero_grads = jax.tree.map(jnp.zeros_like, params)
    totals, (outputs, in_grads, pool_grads) = lax.scan(one_bucket, zero_grads, (inputs_all, pool_all, assign_all, lengths, cotangent_all))
    hidden_out = outputs.reshape(TOKENS, D).astype(jnp.bfloat16)
    input_grad = in_grads.reshape(TOKENS, D)
    neighbour_grad = pool_grads.reshape(BUCKETS * POOL, NBR_LEN, D)
    return (hidden_out, input_grad, neighbour_grad, totals[0], totals[1], totals[2], totals[3], totals[4], totals[5], totals[6], totals[7], totals[8], totals[9], totals[10], totals[11], totals[12], totals[13])
```

```python
from functools import partial

import jax
import jax.numpy as jnp
from jax import lax
from jax.experimental import pallas as pl
from jax.experimental.pallas import tpu as pltpu
from jax.sharding import PartitionSpec as P

HEAD_DIM = 64
SPAN = 64
GROUPS = 16
EPSILON = 1e-05
SCALE = 0.125
MASKED = -1e30
MESH = pl.DeviceIdType.MESH
BF = jnp.bfloat16
F32 = jnp.float32
SMALL_ROWS = 32


def dot(a, b):
    return jnp.dot(a, b, preferred_element_type=F32)


def dot_nt(a, b):
    return lax.dot_general(a, b, (((1,), (1,)), ((), ())), preferred_element_type=F32)


def dot_tn(a, b):
    return lax.dot_general(a, b, (((0,), (0,)), ((), ())), preferred_element_type=F32)


def column_sum(values):
    return jnp.sum(values.astype(F32), axis=0, keepdims=True)


def gelu_parts(a):
    phi = 0.5 * (1.0 + lax.erf(a * 0.7071067811865476))
    density = 0.3989422804014327 * jnp.exp(-0.5 * a * a)
    return a * phi, phi + a * density


def kernel(n_dp, *refs):
    (
        hidden, cot, n_ref, assign, gain, bias, sa_b, sa_ob, ca_b, ca_ob, in_b, out_b,
        w_sa_qkv, w_sa_out, w_ca_qkv, w_ca_out, w_in, w_out,
        hid_o, grad_o, nbr_o, ga_o, gm_o, small_o,
        units, wo, win, wout, nsel, ag, us, xh, rstd, qs, ks, vs, os_, cq, ck, cv,
        lse, gp, dqk, dvs, dkn, dvn, dos, xs, xr, ns, nr, rx0, rx1, rx2, rx3,
        acc_i, acc_o, zst, rz0, rz1, sm, rsm, sel, hbuf,
        lsem, ssem, rsem,
    ) = refs
    rows, dim = hidden.shape
    width = wo.shape[1]
    ff = win.shape[2]
    block = dim // GROUPS
    half = rows // 2
    i = lax.axis_index("dp")
    t = lax.axis_index("tensor")
    m = n_dp // GROUPS
    g = i // m
    r = i % m
    x = g % 2
    y = (g // 2) % 2
    z0 = (g // 4) % 2
    z1 = g // 8
    px = ((g + 1 - 2 * x) * m + r, t)
    py = ((g + 2 - 4 * y) * m + r, t)
    pxy = ((g + 3 - 2 * x - 4 * y) * m + r, t)
    pz0 = ((g + 4 - 8 * z0) * m + r, t)
    pz1 = ((g + 8 - 16 * z1) * m + r, t)
    sib = (i, 1 - t)
    count = [0, 0]
    sends = []

    def load(src, dst):
        copy = pltpu.make_async_copy(src, dst, lsem.at[count[0]])
        count[0] += 1
        copy.start()
        return copy

    def push(src, dst, to):
        k = count[1]
        count[1] += 1
        copy = pltpu.make_async_remote_copy(
            src_ref=src, dst_ref=dst, send_sem=ssem.at[k], recv_sem=rsem.at[k],
            device_id=to, device_id_type=MESH,
        )
        copy.start()
        sends.append(copy)
        return copy

    loads = {}

    def load_attention(layer, src):
        loads[layer, "qkv"] = [
            load(src(0), units.at[layer, 0, :, :, :, :, :, pl.ds(0, width)]),
            load(src(1), units.at[layer, 0, :, :, :, :, :, pl.ds(width, width)]),
            load(src(2), units.at[layer, 1, :, :, :, :, :, pl.ds(0, width)]),
        ]

    load_attention(0, lambda c: w_sa_qkv.at[0, c])
    loads[0, "out"] = [load(w_sa_out.at[0], wo.at[0])]
    load_attention(1, lambda c: w_ca_qkv.at[c])
    loads["n"] = [load(n_ref, nsel)]
    loads[1, "out"] = [load(w_ca_out, wo.at[1])]
    loads["mlp0"] = [load(w_in.at[0], win.at[0]), load(w_out.at[0], wout.at[0])]
    load_attention(2, lambda c: w_sa_qkv.at[1, c])
    loads[2, "out"] = [load(w_sa_out.at[1], wo.at[2])]
    loads["mlp1"] = [load(w_in.at[1], win.at[1]), load(w_out.at[1], wout.at[1])]

    def arrived(key):
        for copy in loads[key]:
            copy.wait()

    barrier = pltpu.get_barrier_semaphore()
    partners = (sib, px, py, pxy, pz0, pz1)
    for to in partners:
        pl.semaphore_signal(barrier, inc=1, device_id=to, device_id_type=MESH)
    pl.semaphore_wait(barrier, len(partners))

    def unit(layer, which, first, size):
        value = units[layer, which, :, :, :, :, :, pl.ds(first, size)]
        return value.reshape(dim, size)

    def unit_store(layer, which, first, value):
        size = value.shape[1]
        units[layer, which, :, :, :, :, :, pl.ds(first, size)] = value.astype(BF).reshape(
            2, 2, 2, 2, block, size
        )

    ex = [0]
    ex_copy = {}

    def exchange_start(part):
        k = ex[0]
        ex[0] += 1
        slot = k % 2
        if k >= 2:
            ex_copy[k - 2].wait_send()
        xs[slot] = part.astype(BF)
        copy = pltpu.make_async_remote_copy(
            src_ref=xs.at[slot], dst_ref=xr.at[slot], send_sem=ssem.at[120 + slot],
            recv_sem=rsem.at[120 + slot], device_id=sib, device_id_type=MESH,
        )
        copy.start()
        ex_copy[k] = copy
        return k

    def exchange_wait(k):
        ex_copy[k].wait_recv()
        return xs[k % 2].astype(F32) + xr[k % 2].astype(F32)

    gathers = {}

    def gather_start(a):
        mine = pl.ds(pl.multiple_of(t * half, half), half)
        gathers[a] = [
            push(ag.at[a, 0, mine], ag.at[a, p + 1, mine], to)
            for p, to in enumerate((px, py, pxy))
        ]

    def gather_relay(a):
        mine = pl.ds(pl.multiple_of(t * half, half), half)
        relays = []
        for p in range(3):
            gathers[a][p].wait_recv()
            relays.append(push(ag.at[a, p + 1, mine], ag.at[a, p + 1, mine], sib))
        gathers[a] = relays

    def gather_wait(a):
        for copy in gathers[a]:
            copy.wait_recv()

    scatter = {}

    def scatter_start(layer, which):
        src = (
            units.at[layer, 0, :, :, :, 1 - x] if which == 0 else units.at[layer, 1, :, :, 1 - y]
        )
        scatter[layer, which] = push(src, rx0.at[layer, which], px if which == 0 else py)

    def scatter_one(layer, which):
        scatter[layer, which].wait_recv()
        got = rx0[layer, which].astype(F32)
        if which == 0:
            units[layer, 0, :, :, :, x] = (units[layer, 0, :, :, :, x].astype(F32) + got).astype(BF)
            src, to = units.at[layer, 0, :, :, 1 - y, x], py
        else:
            units[layer, 1, :, :, y] = (units[layer, 1, :, :, y].astype(F32) + got).astype(BF)
            src, to = units.at[layer, 1, :, :, y, 1 - x], px
        scatter[layer, which] = push(src, rx1.at[layer, which], to)

    def scatter_two(layer, which):
        scatter[layer, which].wait_recv()
        units[layer, which, :, :, y, x] = (
            units[layer, which, :, :, y, x].astype(F32) + rx1[layer, which].astype(F32)
        ).astype(BF)
        scatter[layer, which] = push(
            units.at[layer, which, :, 1 - z0, y, x], rx2.at[layer, which], pz0
        )

    def scatter_three(layer, which):
        scatter[layer, which].wait_recv()
        units[layer, which, :, z0, y, x] = (
            units[layer, which, :, z0, y, x].astype(F32) + rx2[layer, which].astype(F32)
        ).astype(BF)
        scatter[layer, which] = push(
            units.at[layer, which, 1 - z1, z0, y, x], rx3.at[layer, which], pz1
        )

    def scatter_end(layer, which):
        scatter[layer, which].wait_recv()
        ga_o[layer, which] = units[layer, which, z1, z0, y, x].astype(F32) + rx3[
            layer, which
        ].astype(F32)

    def both(step, layer):
        step(layer, 0)
        step(layer, 1)

    def norm_forward(k, store):
        h = hbuf[...]
        centred = h - jnp.mean(h, axis=-1, keepdims=True)
        rec = lax.rsqrt(jnp.mean(centred * centred, axis=-1, keepdims=True) + EPSILON)
        normed = centred * rec
        xh[k] = normed.astype(BF)
        rstd[k] = rec
        store((normed * gain[k : k + 1, :] + bias[k : k + 1, :]).astype(BF))

    def norm_backward(k, dy):
        normed = xh[k].astype(F32)
        sm[k : k + 1, :] = jnp.sum(dy * normed, axis=0, keepdims=True)
        sm[5 + k : 6 + k, :] = jnp.sum(dy, axis=0, keepdims=True)
        scaled = dy * gain[k : k + 1, :]
        first = jnp.mean(scaled, axis=-1, keepdims=True)
        second = jnp.mean(scaled * normed, axis=-1, keepdims=True)
        hbuf[...] += rstd[k] * (scaled - first - normed * second)

    def into_us(k):
        def store(value):
            us[k] = value

        return store

    def into_ag(a):
        def store(value):
            ag[a, 0] = value

        return store

    def stacked(pair):
        lane = lax.broadcasted_iota(jnp.int32, pair.shape, 1)
        zero = jnp.zeros_like(pair)
        return jnp.concatenate(
            [jnp.where(lane < HEAD_DIM, pair, zero), jnp.where(lane < HEAD_DIM, zero, pair)],
            axis=0,
        )

    def merged(both_heads):
        count_rows = both_heads.shape[0] // 2
        lane = lax.broadcasted_iota(jnp.int32, (count_rows, both_heads.shape[1]), 1)
        return jnp.where(lane < HEAD_DIM, both_heads[:count_rows], both_heads[count_rows:])

    pairs = width // (2 * HEAD_DIM)

    def softmax(scores):
        top = jnp.max(scores, axis=-1, keepdims=True)
        terms = jnp.exp(scores - top)
        total = jnp.sum(terms, axis=-1, keepdims=True)
        return terms / total, top + jnp.log(total)

    def causal(scores):
        row_ids = lax.broadcasted_iota(jnp.int32, (rows, rows), 0)
        col_ids = lax.broadcasted_iota(jnp.int32, (rows, rows), 1)
        keep = col_ids <= row_ids
        return jnp.where(jnp.concatenate([keep, keep], axis=0), scores, MASKED)

    def self_forward(j):
        layer = 2 * j
        arrived((layer, "qkv"))
        u = us[layer]
        qk = dot(u, unit(layer, 0, 0, 2 * width))
        qs[j] = (qk[:, :width] + sa_b[2 * j : 2 * j + 1, :]).astype(BF) * BF(SCALE)
        ks[j] = qk[:, width:].astype(BF)
        vs[j] = (dot(u, unit(layer, 1, 0, width)) + sa_b[2 * j + 1 : 2 * j + 2, :]).astype(BF)
        for p in range(pairs):
            cut = slice(2 * HEAD_DIM * p, 2 * HEAD_DIM * (p + 1))
            weights, total = softmax(causal(dot_nt(stacked(qs[j, :, cut]), ks[j, :, cut])))
            lse[j, :, 2 * p : 2 * p + 1] = total[:rows]
            lse[j, :, 2 * p + 1 : 2 * p + 2] = total[rows:]
            os_[layer, :, cut] = merged(dot(weights.astype(BF), vs[j, :, cut])).astype(BF)
        arrived((layer, "out"))
        return exchange_start(dot(os_[layer], wo[layer]))

    def self_backward(j):
        layer = 2 * j
        low = hbuf[...].astype(BF)
        sm[10 + j : 11 + j, :] = column_sum(low)
        dos[...] = dot_nt(low, wo[layer]).astype(BF)
        for p in range(pairs):
            cut = slice(2 * HEAD_DIM * p, 2 * HEAD_DIM * (p + 1))
            q2 = stacked(qs[j, :, cut])
            do2 = stacked(dos[:, cut])
            scores = causal(dot_nt(q2, ks[j, :, cut]))
            total = jnp.concatenate(
                [lse[j, :, 2 * p : 2 * p + 1], lse[j, :, 2 * p + 1 : 2 * p + 2]], axis=0
            )
            weights = jnp.exp(scores - total)
            grads = dot_nt(do2, vs[j, :, cut])
            inner = jnp.sum(weights * grads, axis=-1, keepdims=True)
            score_grad = (weights * (grads - inner)).astype(BF)
            dqk[:, cut] = (SCALE * merged(dot(score_grad, ks[j, :, cut]))).astype(BF)
            dqk[:, slice(width + cut.start, width + cut.stop)] = dot_tn(score_grad, q2).astype(BF)
            dvs[:, cut] = dot_tn(weights.astype(BF), do2).astype(BF)
        sm[16 + 2 * j : 17 + 2 * j, :width] = column_sum(dqk[:, :width])
        sm[17 + 2 * j : 18 + 2 * j, :width] = column_sum(dvs[...])
        k = exchange_start(
            dot_nt(dqk[...], unit(layer, 0, 0, 2 * width))
            + dot_nt(dvs[...], unit(layer, 1, 0, width))
        )
        unit_store(layer, 0, 0, dot_tn(us[layer], dqk[...]))
        scatter_start(layer, 0)
        unit_store(layer, 1, 0, dot_tn(us[layer], dvs[...]))
        unit_store(layer, 1, width, dot_tn(low, os_[layer]))
        scatter_start(layer, 1)
        norm_backward(3 * j, exchange_wait(k))

    spans = rows // SPAN
    keys = nsel.shape[0] // spans

    def shift_up(values):
        moved = pltpu.roll(values, rows - (SPAN - 1), 0)
        row_ids = lax.broadcasted_iota(jnp.int32, values.shape, 0)
        return jnp.where(row_ids < rows - (SPAN - 1), moved, 0.0)

    def shift_down(values):
        moved = pltpu.roll(values, SPAN - 1, 0)
        row_ids = lax.broadcasted_iota(jnp.int32, values.shape, 0)
        return jnp.where(row_ids >= SPAN - 1, moved, 0.0)

    def cross_keys():
        arrived((1, "qkv"))
        arrived("n")
        ck[...] = dot(nsel[...], unit(1, 0, width, width)).astype(BF)
        cv[...] = (dot(nsel[...], unit(1, 1, 0, width)) + ca_b[1:2, :]).astype(BF)

    def cross_forward():
        q = dot(us[1], unit(1, 0, 0, width)) + ca_b[0:1, :]
        cq[...] = shift_up(q).astype(BF) * BF(SCALE)
        outs = []
        for c in range(spans):
            own = slice(c * SPAN, (c + 1) * SPAN)
            span_keys = slice(c * keys, (c + 1) * keys)
            parts = []
            for p in range(pairs):
                cut = slice(2 * HEAD_DIM * p, 2 * HEAD_DIM * (p + 1))
                weights, total = softmax(dot_nt(stacked(cq[own, cut]), ck[span_keys, cut]))
                lse[2, own, 2 * p : 2 * p + 1] = total[:SPAN]
                lse[2, own, 2 * p + 1 : 2 * p + 2] = total[SPAN:]
                parts.append(merged(dot(weights.astype(BF), cv[span_keys, cut])))
            outs.append(jnp.concatenate(parts, axis=1))
        os_[1] = shift_down(jnp.concatenate(outs, axis=0)).astype(BF)
        arrived((1, "out"))
        return exchange_start(dot(os_[1], wo[1]))

    def cross_backward():
        low = hbuf[...].astype(BF)
        sm[12:13, :] = column_sum(low)
        dos[...] = shift_up(dot_nt(low, wo[1])).astype(BF)
        query_grads = []
        for c in range(spans):
            own = slice(c * SPAN, (c + 1) * SPAN)
            span_keys = slice(c * keys, (c + 1) * keys)
            parts = []
            for p in range(pairs):
                cut = slice(2 * HEAD_DIM * p, 2 * HEAD_DIM * (p + 1))
                q2 = stacked(cq[own, cut])
                do2 = stacked(dos[own, cut])
                scores = dot_nt(q2, ck[span_keys, cut])
                total = jnp.concatenate(
                    [lse[2, own, 2 * p : 2 * p + 1], lse[2, own, 2 * p + 1 : 2 * p + 2]], axis=0
                )
                weights = jnp.exp(scores - total)
                grads = dot_nt(do2, cv[span_keys, cut])
                inner = jnp.sum(weights * grads, axis=-1, keepdims=True)
                score_grad = (weights * (grads - inner)).astype(BF)
                parts.append(SCALE * merged(dot(score_grad, ck[span_keys, cut])))
                dkn[span_keys, cut] = dot_tn(score_grad, q2).astype(BF)
                dvn[span_keys, cut] = dot_tn(weights.astype(BF), do2).astype(BF)
            query_grads.append(jnp.concatenate(parts, axis=1))
        dqk[:, :width] = shift_down(jnp.concatenate(query_grads, axis=0)).astype(BF)
        sm[20:21, :width] = column_sum(dqk[:, :width])
        sm[21:22, :width] = column_sum(dvn[...])
        k = exchange_start(dot_nt(dqk[:, :width], unit(1, 0, 0, width)))

        def feature_half(which):
            key_rows = units[1, 0, which, :, :, :, :, pl.ds(width, width)].reshape(dim // 2, width)
            value_rows = units[1, 1, which, :, :, :, :, pl.ds(0, width)].reshape(dim // 2, width)
            return dot_nt(dkn[...], key_rows) + dot_nt(dvn[...], value_rows)

        ns[...] = feature_half(1 - t).astype(BF)
        other = push(ns, nr, sib)
        nbr_keep = feature_half(t).astype(BF)
        nbr_sum[0] = (other, nbr_keep)
        unit_store(1, 0, 0, dot_tn(us[1], dqk[:, :width]))
        unit_store(1, 0, width, dot_tn(nsel[...], dkn[...]))
        scatter_start(1, 0)
        unit_store(1, 1, 0, dot_tn(nsel[...], dvn[...]))
        unit_store(1, 1, width, dot_tn(low, os_[1]))
        scatter_start(1, 1)
        norm_backward(1, exchange_wait(k))

    nbr_sum = [None]

    def neighbours_end():
        other, keep = nbr_sum[0]
        other.wait_recv()
        nsel_rows = nsel.shape[0]
        pool = nbr_o.shape[0]
        length = nsel_rows // pool
        total = keep.astype(F32) + nr[...].astype(F32)
        for slot in range(pool):
            summed = jnp.zeros((length, total.shape[1]), F32)
            for pick in range(pool):
                hit = jnp.where(assign[pick] == slot, F32(1.0), F32(0.0))
                summed += hit * total[pick * length : (pick + 1) * length]
            nbr_o[slot] = summed

    cuts = [slice(c * dim, (c + 1) * dim) for c in range(ff // dim)]

    def mlp_forward(j):
        arrived("mlp%d" % j)
        part = None
        for cut in cuts:
            pre = dot(ag[2 * j, 0], win[j, :, cut]) + in_b[j : j + 1, cut]
            active, slope = gelu_parts(pre)
            gp[j, :, cut] = slope.astype(BF)
            term = dot(active.astype(BF), wout[j, cut, :])
            part = term if part is None else part + term
        return exchange_start(part)

    def mlp_backward(j):
        low = ag[2 * j + 1, 0]
        sm[13 + j : 14 + j, :] = column_sum(low)
        part = None
        for c, cut in enumerate(cuts):
            down = dot_nt(low, wout[j, cut, :])
            pre_grad = (down * gp[j, :, cut].astype(F32)).astype(BF)
            sm[24 + 2 * j + c : 25 + 2 * j + c, :] = column_sum(pre_grad)
            term = dot_nt(pre_grad, win[j, :, cut])
            part = term if part is None else part + term
        k = exchange_start(part)
        return k

    def mlp_weights(j):
        gather_wait(2 * j)
        gather_wait(2 * j + 1)

        acc_i[...] = jnp.zeros_like(acc_i)
        acc_o[...] = jnp.zeros_like(acc_o)

        def bucket(b, carry):
            u = ag[2 * j, b]
            d = ag[2 * j + 1, b]
            u_rows = dot_nt(sel[...], u).astype(BF)
            d_rows = dot_nt(sel[...], d).astype(BF)
            for cut in cuts:
                pre = dot(u, win[j, :, cut]) + in_b[j : j + 1, cut]
                active, slope = gelu_parts(pre)
                pre_grad = (dot_nt(d, wout[j, cut, :]) * slope).astype(BF)
                acc_i[:, cut] += dot(u_rows, pre_grad)
                acc_o[:, cut] += dot(d_rows, active.astype(BF))
            return carry

        lax.fori_loop(0, 4, bucket, 0)
        zst[j, 0] = acc_i[...].astype(BF).reshape(2, 2, block, ff)
        zst[j, 1] = acc_o[...].astype(BF).reshape(2, 2, block, ff)
        scatter["z", j] = push(zst.at[j, :, :, 1 - z0], rz0.at[j], pz0)

    def mlp_one(j):
        scatter["z", j].wait_recv()
        zst[j, :, :, z0] = (zst[j, :, :, z0].astype(F32) + rz0[j].astype(F32)).astype(BF)
        scatter["z", j] = push(zst.at[j, :, 1 - z1, z0], rz1.at[j], pz1)

    def mlp_end(j):
        scatter["z", j].wait_recv()
        gm_o[j] = zst[j, :, z1, z0].astype(F32) + rz1[j].astype(F32)

    ag[3, 0] = cot[...]
    gather_start(3)
    sm[...] = jnp.zeros_like(sm)
    hbuf[...] = hidden[...].astype(F32)
    row_ids = lax.broadcasted_iota(jnp.int32, (block, dim), 0)
    col_ids = lax.broadcasted_iota(jnp.int32, (block, dim), 1)
    for q in range(4):
        shift = q * 4 * block + (g % 4) * block
        sel[q * block : (q + 1) * block, :] = jnp.where(col_ids == row_ids + shift, 1.0, 0.0).astype(BF)

    norm_forward(0, into_us(0))
    k = self_forward(0)
    cross_keys()
    hbuf[...] += exchange_wait(k) + sa_ob[0:1, :]
    norm_forward(1, into_us(1))
    k = cross_forward()
    hbuf[...] += exchange_wait(k) + ca_ob[...]
    norm_forward(2, into_ag(0))
    gather_start(0)
    k = mlp_forward(0)
    hbuf[...] += exchange_wait(k) + out_b[0:1, :]
    norm_forward(3, into_us(2))
    gather_relay(3)
    k = self_forward(1)
    hbuf[...] += exchange_wait(k) + sa_ob[1:2, :]
    norm_forward(4, into_ag(2))
    gather_start(2)
    k = mlp_forward(1)
    hid_o[...] = (hbuf[...] + exchange_wait(k) + out_b[1:2, :]).astype(BF)
    hbuf[...] = cot[...].astype(F32)

    k = mlp_backward(1)
    gather_relay(0)
    norm_backward(4, exchange_wait(k))
    self_backward(1)
    gather_relay(2)
    ag[1, 0] = hbuf[...].astype(BF)
    gather_start(1)
    mlp_weights(1)
    k = mlp_backward(0)
    both(scatter_one, 2)
    norm_backward(2, exchange_wait(k))
    cross_backward()
    both(scatter_two, 2)
    gather_relay(1)
    mlp_one(1)
    self_backward(0)
    grad_o[...] = hbuf[...]
    small_copy = []

    def small_step(k, to):
        if k:
            small_copy[-1].wait_recv()
            sm_next = sm_stage[k - 1][...] + rsm[k - 1]
            small_bufs[k][...] = sm_next
        small_copy.append(push(small_bufs[k], rsm.at[k], to))

    small_bufs = [sm] + [small_o.at[q] for q in range(3)]
    sm_stage = small_bufs
    small_step(0, px)
    both(scatter_three, 2)
    mlp_weights(0)
    small_step(1, py)
    both(scatter_one, 1)
    neighbours_end()
    small_step(2, pz0)
    both(scatter_one, 0)
    both(scatter_end, 2)
    small_step(3, pz1)
    both(scatter_two, 1)
    mlp_end(1)
    mlp_one(0)
    both(scatter_two, 0)
    both(scatter_three, 1)
    small_copy[-1].wait_recv()
    small_o[3] = small_bufs[3][...] + rsm[3]
    both(scatter_three, 0)
    both(scatter_end, 1)
    mlp_end(0)
    both(scatter_end, 0)
    for copy in sends:
        copy.wait_send()
    for k in (ex[0] - 2, ex[0] - 1):
        ex_copy[k].wait_send()


def on_device(
    n_dp,
    hidden_in, lengths, neighbours, assign, cotangent, norm_gain, norm_bias, sa_qkv, sa_bias,
    sa_out, sa_out_bias, ca_qkv, ca_bias, ca_out, ca_out_bias, mlp_in, mlp_in_bias, mlp_out,
    mlp_out_bias,
):
    rows, dim = hidden_in.shape
    width = sa_out.shape[1]
    ff = mlp_in.shape[2]
    pool, length = neighbours.shape[0], neighbours.shape[1]
    block = dim // GROUPS
    picks = assign.size * length
    live = (jnp.arange(rows, dtype=jnp.int32) < lengths[0])[:, None]
    cot = jnp.where(live, cotangent, jnp.zeros_like(cotangent))
    flat = assign.reshape(-1)
    picked = neighbours[flat].reshape(picks, dim)
    vmem = pl.BlockSpec(memory_space=pltpu.VMEM)
    smem = pl.BlockSpec(memory_space=pltpu.SMEM)
    hbm = pl.BlockSpec(memory_space=pl.ANY)
    sa_w = sa_qkv.reshape(2, 3, 2, 2, 2, 2, block, width)
    ca_w = ca_qkv.reshape(3, 2, 2, 2, 2, block, width)
    outs = (
        jax.ShapeDtypeStruct((rows, dim), BF),
        jax.ShapeDtypeStruct((rows, dim), F32),
        jax.ShapeDtypeStruct((pool, length, width), F32),
        jax.ShapeDtypeStruct((3, 2, block, 2 * width), F32),
        jax.ShapeDtypeStruct((2, 2, block, ff), F32),
        jax.ShapeDtypeStruct((4, SMALL_ROWS, dim), F32),
    )
    V = pltpu.VMEM
    scratch = [
        V((3, 2, 2, 2, 2, 2, block, 2 * width), BF),
        V((3, width, dim), BF),
        V((2, dim, ff), BF),
        V((2, ff, dim), BF),
        V((picks, dim), BF),
        V((4, 4, rows, dim), BF),
        V((3, rows, dim), BF),
        V((5, rows, dim), BF),
        V((5, rows, 1), F32),
        V((2, rows, width), BF),
        V((2, rows, width), BF),
        V((2, rows, width), BF),
        V((3, rows, width), BF),
        V((rows, width), BF),
        V((picks, width), BF),
        V((picks, width), BF),
        V((3, rows, 128), F32),
        V((2, rows, ff), BF),
        V((rows, 2 * width), BF),
        V((rows, width), BF),
        V((picks, width), BF),
        V((picks, width), BF),
        V((rows, width), BF),
        V((2, rows, dim), BF),
        V((2, rows, dim), BF),
        V((picks, width), BF),
        V((picks, width), BF),
        V((3, 2, 2, 2, 2, block, 2 * width), BF),
        V((3, 2, 2, 2, block, 2 * width), BF),
        V((3, 2, 2, block, 2 * width), BF),
        V((3, 2, block, 2 * width), BF),
        V((4 * block, ff), F32),
        V((4 * block, ff), F32),
        V((2, 2, 2, 2, block, ff), BF),
        V((2, 2, 2, block, ff), BF),
        V((2, 2, block, ff), BF),
        V((SMALL_ROWS, dim), F32),
        V((4, SMALL_ROWS, dim), F32),
        V((4 * block, dim), BF),
        V((rows, dim), F32),
        pltpu.SemaphoreType.DMA((32,)),
        pltpu.SemaphoreType.DMA((128,)),
        pltpu.SemaphoreType.DMA((128,)),
    ]
    hid, grad, nbr, ga, gm, small = pl.pallas_call(
        partial(kernel, n_dp),
        out_shape=outs,
        in_specs=[vmem, vmem, hbm, smem] + [vmem] * 8 + [hbm] * 6,
        out_specs=(vmem,) * 6,
        scratch_shapes=scratch,
        compiler_params=pltpu.CompilerParams(
            collective_id=0, has_side_effects=True, vmem_limit_bytes=64 * 1024 * 1024 - 65536
        ),
    )(
        hidden_in, cot, picked, flat, norm_gain, norm_bias, sa_bias.reshape(4, width), sa_out_bias,
        ca_bias, ca_out_bias.reshape(1, dim), mlp_in_bias, mlp_out_bias,
        sa_w, sa_out, ca_w, ca_out, mlp_in, mlp_out,
    )
    small = small[3]
    rest = n_dp // GROUPS
    if rest > 1:
        members = [[a * rest + b for b in range(rest)] for a in range(GROUPS)]
        ga = lax.psum_scatter(ga, "dp", scatter_dimension=2, axis_index_groups=members, tiled=True)
        gm = lax.psum_scatter(gm, "dp", scatter_dimension=2, axis_index_groups=members, tiled=True)
        small = lax.psum(small, "dp", axis_index_groups=members)
    sa_qkv_grad = jnp.stack(
        [
            jnp.stack([ga[a, 0, :, :width], ga[a, 0, :, width:], ga[a, 1, :, :width]])
            for a in (0, 2)
        ]
    )
    ca_qkv_grad = jnp.stack([ga[1, 0, :, :width], ga[1, 0, :, width:], ga[1, 1, :, :width]])
    sa_out_grad = jnp.stack([ga[0, 1, :, width:].T, ga[2, 1, :, width:].T])
    ca_out_grad = ga[1, 1, :, width:].T
    mlp_in_grad = gm[:, 0]
    mlp_out_grad = gm[:, 1].swapaxes(1, 2)
    return (
        jnp.where(live, hid, jnp.zeros_like(hid)),
        grad,
        nbr,
        small[0:5],
        small[5:10],
        sa_qkv_grad,
        small[16:20, :width].reshape(2, 2, width),
        sa_out_grad,
        small[10:12],
        ca_qkv_grad,
        small[20:22, :width],
        ca_out_grad,
        small[12],
        mlp_in_grad,
        small[24:28].reshape(2, ff),
        mlp_out_grad,
        small[13:15],
    )


def solution(mesh):
    return jax.shard_map(
        partial(on_device, mesh.shape["dp"]),
        mesh=mesh,
        in_specs=(
            P("dp", None),
            P("dp"),
            P("dp", None, None),
            P("dp", None),
            P("dp", None),
            P(),
            P(),
            P(None, None, None, "tensor"),
            P(None, None, "tensor"),
            P(None, "tensor", None),
            P(),
            P(None, None, "tensor"),
            P(None, "tensor"),
            P("tensor", None),
            P(),
            P(None, None, "tensor"),
            P(None, "tensor"),
            P(None, "tensor", None),
            P(),
        ),
        out_specs=(
            P("dp", None),
            P("dp", None),
            P("dp", None, "tensor"),
            P(),
            P(),
            P(None, None, "dp", "tensor"),
            P(None, None, "tensor"),
            P(None, "tensor", "dp"),
            P(),
            P(None, "dp", "tensor"),
            P(None, "tensor"),
            P("tensor", "dp"),
            P(),
            P(None, "dp", "tensor"),
            P(None, "tensor"),
            P(None, "tensor", "dp"),
            P(),
        ),
        check_vma=False,
    )
```

```python
from functools import partial

import jax
import jax.numpy as jnp
from jax import lax
from jax.experimental import pallas as pl
from jax.experimental.pallas import tpu as pltpu
from jax.sharding import PartitionSpec as P

HEAD_DIM = 64
SPAN = 64
GROUPS = 16
EPSILON = 1e-05
SCALE = 0.125
MASKED = -1e30
MESH = pl.DeviceIdType.MESH
BF = jnp.bfloat16
F32 = jnp.float32
SMALL_ROWS = 32
ORDER = (
    "b1", "S2", "d1", "b0", "g2", "C", "gru1", "gswd1", "gswu2", "gswd2", "rf2", "Cn", "rows0",
    "Cv", "mw00", "rf1", "s1b2", "mw01", "s1a2", "Ck", "rows1", "S0", "mz21", "s221", "mz20",
    "s1b1", "s220", "s1a1", "rf0", "s1b0", "nbr", "sm0", "mw11", "s210", "mz30", "s321", "s320",
    "mw10", "s421", "s1a0", "mz31", "s310", "s211", "s420", "s201", "s311", "ms1", "se21", "sm1",
    "se20", "s410", "s200", "mze0", "s301", "se10", "s411", "sm2", "ms0", "s300", "sm3", "s401",
    "se01", "s400", "me0", "mze1", "se11", "me1", "sm4", "se00",
)


def dot(a, b):
    return jnp.dot(a, b, preferred_element_type=F32)


def dot_nt(a, b):
    return lax.dot_general(a, b, (((1,), (1,)), ((), ())), preferred_element_type=F32)


def dot_tn(a, b):
    return lax.dot_general(a, b, (((0,), (0,)), ((), ())), preferred_element_type=F32)


def column_sum(values):
    return jnp.sum(values.astype(F32), axis=0, keepdims=True)


def gelu_parts(a):
    phi = 0.5 * (1.0 + lax.erf(a * 0.7071067811865476))
    density = 0.3989422804014327 * jnp.exp(-0.5 * a * a)
    return a * phi, phi + a * density


def kernel(n_dp, *refs):
    (
        lengths, assign, gain, bias, sa_b, sa_ob, ca_b, ca_ob, in_b, out_b,
        hidden, cot, n_ref, w_sa_qkv, w_sa_out, w_ca_qkv, w_ca_out, w_in, w_out,
        hid_h, grad_h, nbr_h, ga_h, gm_h, small_h,
        hid_o, nbr_o, ga_o, gm_o, small_o,
        units, wo, win, wout, nsel, ag, us, xh, rstd, qs, ks, vs, os_, cq, ck, cv,
        lse, gp, dqk, dvs, dkn, dvn, dos, xs, xr, rx0, rx1, rx2,
        acc, zst, rz, rw0, rw1, sm, rsm, hbuf,
        ut, dt, rut_x, rut_y, rdt, ro, rdqk, rdv, turned, turned_rows,
        lsem, ssem, rsem,
    ) = refs
    rows, dim = hbuf.shape
    width = wo.shape[1]
    ff = win.shape[2]
    block = dim // GROUPS
    half = rows // 2
    i = lax.axis_index("dp")
    t = lax.axis_index("tensor")
    m = n_dp // GROUPS
    g = i // m
    r = i % m
    x = g % 2
    y = (g // 2) % 2
    z0 = (g // 4) % 2
    z1 = g // 8
    px = ((g + 1 - 2 * x) * m + r, t)
    py = ((g + 2 - 4 * y) * m + r, t)
    pxy = ((g + 3 - 2 * x - 4 * y) * m + r, t)
    pz0 = ((g + 4 - 8 * z0) * m + r, t)
    pz1 = ((g + 8 - 16 * z1) * m + r, t)
    pz = ((g + 12 - 8 * z0 - 16 * z1) * m + r, t)
    zz = g // 4
    sib = (i, 1 - t)
    count = [0, 0]
    sends = []

    def load(src, dst):
        copy = pltpu.make_async_copy(src, dst, lsem.at[count[0]])
        count[0] += 1
        copy.start()
        return copy

    stores = []

    def store(src, dst):
        stores.append(load(src, dst))

    def push(src, dst, to):
        k = count[1]
        count[1] += 1
        copy = pltpu.make_async_remote_copy(
            src_ref=src, dst_ref=dst, send_sem=ssem.at[k], recv_sem=rsem.at[k],
            device_id=to, device_id_type=MESH,
        )
        copy.start()
        sends.append(copy)
        return copy

    loads = {}

    def load_attention(layer, src):
        def blocks(c):
            return src(c).reshape(2, 2, 2, 2, block, width)

        loads[layer, "qkv"] = [
            load(blocks(0), units.at[layer, 0, :, :, :, :, :, pl.ds(0, width)]),
            load(blocks(1), units.at[layer, 0, :, :, :, :, :, pl.ds(width, width)]),
            load(blocks(2), units.at[layer, 1, :, :, :, :, :, pl.ds(0, width)]),
        ]

    loads["hidden"] = [load(hidden, dqk.at[0])]
    loads["cot"] = [load(cot, ag.at[3, 0])]
    load_attention(0, lambda c: w_sa_qkv.at[0, c])
    loads[0, "out"] = [load(w_sa_out.at[0], wo.at[0])]
    load_attention(1, lambda c: w_ca_qkv.at[c])
    pool, length = n_ref.shape[0], n_ref.shape[1]
    loads["n"] = [
        load(n_ref.at[:, :, pl.ds(c * width, width)], into.reshape(pool, length, width))
        for c, into in enumerate((dkn, dvn))
    ]
    loads[1, "out"] = [load(w_ca_out, wo.at[1])]
    loads["mlp0"] = [load(w_in.at[0], win.at[0]), load(w_out.at[0], wout.at[0])]
    load_attention(2, lambda c: w_sa_qkv.at[1, c])
    loads[2, "out"] = [load(w_sa_out.at[1], wo.at[2])]
    loads["mlp1"] = [load(w_in.at[1], win.at[1]), load(w_out.at[1], wout.at[1])]

    def arrived(key):
        for copy in loads[key]:
            copy.wait()

    barrier = pltpu.get_barrier_semaphore()
    partners = (sib, px, py, pxy, pz0, pz1, pz)
    for to in partners:
        pl.semaphore_signal(barrier, inc=1, device_id=to, device_id_type=MESH)

    def entered():
        pl.semaphore_wait(barrier, len(partners))

    def unit(layer, which, first, size):
        value = units[layer, which, :, :, :, :, :, pl.ds(first, size)]
        return value.reshape(dim, size)

    def unit_store(layer, which, first, value):
        size = value.shape[1]
        units[layer, which, :, :, :, :, :, pl.ds(first, size)] = value.astype(BF).reshape(
            2, 2, 2, 2, block, size
        )

    ex = [0]
    ex_copy = {}

    def exchange_start(part):
        k = ex[0]
        ex[0] += 1
        slot = k % 2
        if k >= 2:
            ex_copy[k - 2].wait_send()
        xs[slot] = part.astype(BF)
        copy = pltpu.make_async_remote_copy(
            src_ref=xs.at[slot], dst_ref=xr.at[slot], send_sem=ssem.at[158 + slot],
            recv_sem=rsem.at[158 + slot], device_id=sib, device_id_type=MESH,
        )
        copy.start()
        ex_copy[k] = copy
        return k

    def exchange_wait(k):
        ex_copy[k].wait_recv()
        return xs[k % 2].astype(F32) + xr[k % 2].astype(F32)

    gathers = {}

    mine = pl.ds(pl.multiple_of(t * half, half), half)
    quarter = half // 2
    upper = pl.ds(pl.multiple_of(t * half, quarter), quarter)
    lower = pl.ds(pl.multiple_of(t * half + quarter, quarter), quarter)

    def gather_start(a, peers=(px, py)):
        gathers[a] = [
            push(ag.at[a, 0, mine], ag.at[a, p + 1, mine], to) for p, to in enumerate(peers)
        ]

    def gather_swap(a):
        for copy in gathers[a]:
            copy.wait_recv()
        gathers[a] = [push(ag.at[a, p, mine], ag.at[a, p, mine], sib) for p in (1, 2, 3)]

    def gather_forward(a):
        for copy in gathers[a]:
            copy.wait_recv()
        gathers[a] = [
            push(ag.at[a, 1, upper], ag.at[a, 3, upper], py),
            push(ag.at[a, 2, lower], ag.at[a, 3, lower], px),
        ] + [push(ag.at[a, p, mine], ag.at[a, p, mine], sib) for p in (1, 2)]

    def gather_relay(a):
        for copy in gathers[a][:2]:
            copy.wait_recv()
        gathers[a] = gathers[a][2:] + [push(ag.at[a, 3, mine], ag.at[a, 3, mine], sib)]

    def gather_wait(a):
        for copy in gathers[a]:
            copy.wait_recv()

    UP, DOWN = {1: 0, 2: 1, 3: 2}, {0: 3, 1: 4, 2: 0}
    above = ((g + 4) * m + r, t)
    below = ((g - 4) * m + r, t)
    chains = []

    class Chain:
        def __init__(self, shard, into):
            self.base = count[1]
            count[1] += 5
            self.shard, self.into = shard, into
            chains.append(self)

        def copy(self, s, slot, to):
            return pltpu.make_async_remote_copy(
                src_ref=self.shard(s), dst_ref=self.into.at[slot],
                send_sem=ssem.at[self.base + slot], recv_sem=rsem.at[self.base + slot],
                device_id=to, device_id_type=MESH,
            )

        def arrive(self, s, slot):
            self.copy(s, slot, above).wait_recv()
            return self.into[slot].astype(F32)

        def pass_on(self, s, slot, to):
            own = self.shard(s)
            own[...] = (own[...].astype(F32) + self.arrive(s, slot)).astype(BF)
            self.copy(s, slot, to).start()

        def first(self):
            @pl.when(zz == 0)
            def _():
                for s in (3, 2, 1):
                    self.copy(s, UP[s], above).start()

            @pl.when(zz == 3)
            def _():
                for s in (0, 1, 2):
                    self.copy(s, DOWN[s], below).start()

        def second(self):
            @pl.when(zz == 1)
            def _():
                for s in (3, 2):
                    self.pass_on(s, UP[s], above)

            @pl.when(zz == 2)
            def _():
                for s in (0, 1):
                    self.pass_on(s, DOWN[s], below)

        def third(self):
            @pl.when(zz == 2)
            def _():
                self.pass_on(3, UP[3], above)

            @pl.when(zz == 1)
            def _():
                self.pass_on(0, DOWN[0], below)

        def end(self, out):
            for s in range(4):
                @pl.when(zz == s)
                def _(s=s):
                    total = self.shard(s)[...].astype(F32)
                    if s > 0:
                        total += self.arrive(s, UP[s])
                    if s < 3:
                        total += self.arrive(s, DOWN[s])
                    out[...] = total

        def sent(self):
            for z, slots in enumerate(
                ((UP[1], UP[2], UP[3]), (UP[2], UP[3], DOWN[0]),
                 (UP[3], DOWN[0], DOWN[1]), (DOWN[0], DOWN[1], DOWN[2]))
            ):
                @pl.when(zz == z)
                def _(slots=slots):
                    for slot in slots:
                        self.copy(0, slot, above).wait_send()

    def turn(dst, value):
        dst[...] = value.T.reshape(2, 2, 2, 2, block, rows)

    scatter = {}
    factors = {}

    def send_inputs(layer):
        turn(ut.at[layer], us[layer])
        factors[layer, "u0"] = push(ut.at[layer, t, :, :, 1 - x], rut_x.at[layer, t], px)
        if layer != 1:
            factors[layer, "u1"] = push(ut.at[layer, t, :, 1 - y], rut_y.at[layer // 2, t], py)

    def send_attended(layer):
        factors[layer, "o"] = push(os_.at[layer], ro.at[layer], py)

    def send_upstream(layer, low):
        turn(dt.at[layer], low)
        factors[layer, "d"] = push(dt.at[layer, t, :, 1 - y], rdt.at[layer, t], py)

    def relay_factor(layer, name):
        into = {"u0": rut_x.at[layer, t], "u1": rut_y.at[layer // 2, t], "d": rdt.at[layer, t]}
        factors[layer, name].wait_recv()
        factors[layer, name] = push(into[name], into[name], sib)

    def relay_factors(layer):
        relay_factor(layer, "u0")
        if layer != 1:
            relay_factor(layer, "u1")
        relay_factor(layer, "d")

    def send_grads(layer):
        if layer == 1:
            factors[layer, "0"] = push(
                dqk.at[layer, :, pl.ds(0, width)], rdqk.at[layer, :, pl.ds(0, width)], px
            )
        else:
            factors[layer, "0"] = push(dqk.at[layer], rdqk.at[layer], px)
            factors[layer, "1"] = push(dvs.at[layer // 2], rdv.at[layer // 2], py)

    first, second = pl.ds(0, width), pl.ds(width, width)

    def scatter_one(layer, which):
        if which == 0:
            for name in ("u0", "0"):
                factors[layer, name].wait_recv()
            size = width if layer == 1 else 2 * width
            total = dot(ut[layer, :, :, :, x].reshape(dim // 2, rows), dqk[layer, :, :size]) + dot(
                rut_x[layer].reshape(dim // 2, rows), rdqk[layer, :, :size]
            )
            units[layer, 0, :, :, :, x, :, pl.ds(0, size)] = total.astype(BF).reshape(
                2, 2, 2, block, size
            )
            if layer == 1:
                factors["k"].wait_recv()
                units[1, 0, :, :, :, x, :, second] = (
                    units[1, 0, :, :, :, x, :, second].astype(F32) + rx0[0].astype(F32)
                ).astype(BF)
            scatter[layer, 0] = push(units.at[layer, 0, :, :, 1 - y, x], rx1.at[layer, 0], py)
            return
        if layer == 1:
            factors["v"].wait_recv()
            units[1, 1, :, :, y, :, :, first] = (
                units[1, 1, :, :, y, :, :, first].astype(F32) + rx0[1].astype(F32)
            ).astype(BF)
        else:
            for name in ("u1", "1"):
                factors[layer, name].wait_recv()
            total = dot(ut[layer, :, :, y].reshape(dim // 2, rows), dvs[layer // 2]) + dot(
                rut_y[layer // 2].reshape(dim // 2, rows), rdv[layer // 2]
            )
            units[layer, 1, :, :, y, :, :, first] = total.astype(BF).reshape(
                2, 2, 2, block, width
            )
        for name in ("o", "d"):
            factors[layer, name].wait_recv()
        total = dot(dt[layer, :, :, y].reshape(dim // 2, rows), os_[layer]) + dot(
            rdt[layer].reshape(dim // 2, rows), ro[layer]
        )
        units[layer, 1, :, :, y, :, :, second] = total.astype(BF).reshape(2, 2, 2, block, width)
        scatter[layer, 1] = push(units.at[layer, 1, :, :, y, 1 - x], rx1.at[layer, 1], px)

    def scatter_two(layer, which):
        scatter[layer, which].wait_recv()
        units[layer, which, :, :, y, x] = (
            units[layer, which, :, :, y, x].astype(F32) + rx1[layer, which].astype(F32)
        ).astype(BF)
        chain = Chain(
            lambda s: units.at[layer, which, s // 2, s % 2, y, x], rx2.at[layer, which]
        )
        scatter[layer, which] = chain
        chain.first()

    def scatter_three(layer, which):
        scatter[layer, which].second()

    def scatter_four(layer, which):
        scatter[layer, which].third()

    def scatter_end(layer, which):
        scatter[layer, which].end(ga_o.at[layer, which])
        store(ga_o.at[layer, which], ga_h.at[layer, which])

    def norm_forward(k, store):
        h = hbuf[...]
        centred = h - jnp.mean(h, axis=-1, keepdims=True)
        rec = lax.rsqrt(jnp.mean(centred * centred, axis=-1, keepdims=True) + EPSILON)
        normed = centred * rec
        xh[k] = normed.astype(BF)
        rstd[k] = rec
        store((normed * gain[k : k + 1, :] + bias[k : k + 1, :]).astype(BF))

    def norm_backward(k, dy):
        normed = xh[k].astype(F32)
        sm[k : k + 1, :] = jnp.sum(dy * normed, axis=0, keepdims=True)
        sm[5 + k : 6 + k, :] = jnp.sum(dy, axis=0, keepdims=True)
        scaled = dy * gain[k : k + 1, :]
        first = jnp.mean(scaled, axis=-1, keepdims=True)
        second = jnp.mean(scaled * normed, axis=-1, keepdims=True)
        hbuf[...] += rstd[k] * (scaled - first - normed * second)

    def into_us(k):
        def store(value):
            us[k] = value

        return store

    def into_ag(a):
        def store(value):
            ag[a, 0] = value

        return store

    def stacked(pair):
        lane = lax.broadcasted_iota(jnp.int32, pair.shape, 1)
        zero = jnp.zeros_like(pair)
        return jnp.concatenate(
            [jnp.where(lane < HEAD_DIM, pair, zero), jnp.where(lane < HEAD_DIM, zero, pair)],
            axis=0,
        )

    def merged(both_heads):
        count_rows = both_heads.shape[0] // 2
        lane = lax.broadcasted_iota(jnp.int32, (count_rows, both_heads.shape[1]), 1)
        return jnp.where(lane < HEAD_DIM, both_heads[:count_rows], both_heads[count_rows:])

    pairs = width // (2 * HEAD_DIM)

    def softmax(scores):
        top = jnp.max(scores, axis=-1, keepdims=True)
        terms = jnp.exp(scores - top)
        total = jnp.sum(terms, axis=-1, keepdims=True)
        return terms / total, top + jnp.log(total)

    def causal(scores):
        row_ids = lax.broadcasted_iota(jnp.int32, (rows, rows), 0)
        col_ids = lax.broadcasted_iota(jnp.int32, (rows, rows), 1)
        keep = col_ids <= row_ids
        return jnp.where(jnp.concatenate([keep, keep], axis=0), scores, MASKED)

    def self_forward(j):
        layer = 2 * j
        arrived((layer, "qkv"))
        u = us[layer]
        qk = dot(u, unit(layer, 0, 0, 2 * width))
        qs[j] = (qk[:, :width] + sa_b[j, 0:1, :]).astype(BF) * BF(SCALE)
        ks[j] = qk[:, width:].astype(BF)
        vs[j] = (dot(u, unit(layer, 1, 0, width)) + sa_b[j, 1:2, :]).astype(BF)
        for p in range(pairs):
            cut = slice(2 * HEAD_DIM * p, 2 * HEAD_DIM * (p + 1))
            weights, total = softmax(causal(dot_nt(stacked(qs[j, :, cut]), ks[j, :, cut])))
            lse[j, :, 2 * p : 2 * p + 1] = total[:rows]
            lse[j, :, 2 * p + 1 : 2 * p + 2] = total[rows:]
            os_[layer, :, cut] = merged(dot(weights.astype(BF), vs[j, :, cut])).astype(BF)
        arrived((layer, "out"))
        k = exchange_start(dot(os_[layer], wo[layer]))
        send_attended(layer)
        return k

    def self_backward(j):
        layer = 2 * j
        low = hbuf[...].astype(BF)
        send_upstream(layer, low)
        dos[...] = dot_nt(low, wo[layer]).astype(BF)
        for p in range(pairs):
            cut = slice(2 * HEAD_DIM * p, 2 * HEAD_DIM * (p + 1))
            q2 = stacked(qs[j, :, cut])
            do2 = stacked(dos[:, cut])
            scores = causal(dot_nt(q2, ks[j, :, cut]))
            total = jnp.concatenate(
                [lse[j, :, 2 * p : 2 * p + 1], lse[j, :, 2 * p + 1 : 2 * p + 2]], axis=0
            )
            weights = jnp.exp(scores - total)
            grads = dot_nt(do2, vs[j, :, cut])
            inner = jnp.sum(weights * grads, axis=-1, keepdims=True)
            score_grad = (weights * (grads - inner)).astype(BF)
            dqk[layer, :, cut] = (SCALE * merged(dot(score_grad, ks[j, :, cut]))).astype(BF)
            dqk[layer, :, slice(width + cut.start, width + cut.stop)] = dot_tn(
                score_grad, q2
            ).astype(BF)
            dvs[j, :, cut] = dot_tn(weights.astype(BF), do2).astype(BF)
        if j == 0:
            send_grads(layer)
        k = exchange_start(
            dot_nt(dqk[layer], unit(layer, 0, 0, 2 * width))
            + dot_nt(dvs[j], unit(layer, 1, 0, width))
        )
        sm[10 + j : 11 + j, :] = column_sum(low)
        sm[16 + 2 * j : 17 + 2 * j, :width] = column_sum(dqk[layer, :, :width])
        sm[17 + 2 * j : 18 + 2 * j, :width] = column_sum(dvs[j])
        norm_backward(3 * j, exchange_wait(k))

    spans = rows // SPAN
    keys = nsel.shape[0] // spans

    def shift_up(values):
        moved = pltpu.roll(values, rows - (SPAN - 1), 0)
        row_ids = lax.broadcasted_iota(jnp.int32, values.shape, 0)
        return jnp.where(row_ids < rows - (SPAN - 1), moved, 0.0)

    def shift_down(values):
        moved = pltpu.roll(values, SPAN - 1, 0)
        row_ids = lax.broadcasted_iota(jnp.int32, values.shape, 0)
        return jnp.where(row_ids >= SPAN - 1, moved, 0.0)

    def cross_keys():
        arrived((1, "qkv"))
        arrived("n")
        for pick in range(pool):
            own = slice(pick * length, (pick + 1) * length)
            rows_of = pl.ds(assign[pick % 2, pick // 2] * length, length)
            nsel[own, :width] = dkn[rows_of, :]
            nsel[own, width:] = dvn[rows_of, :]
        ck[...] = dot(nsel[...], unit(1, 0, width, width)).astype(BF)
        cv[...] = (dot(nsel[...], unit(1, 1, 0, width)) + ca_b[1:2, :]).astype(BF)

    def cross_forward():
        q = dot(us[1], unit(1, 0, 0, width)) + ca_b[0:1, :]
        cq[...] = shift_up(q).astype(BF) * BF(SCALE)
        outs = []
        for c in range(spans):
            own = slice(c * SPAN, (c + 1) * SPAN)
            span_keys = slice(c * keys, (c + 1) * keys)
            parts = []
            for p in range(pairs):
                cut = slice(2 * HEAD_DIM * p, 2 * HEAD_DIM * (p + 1))
                weights, total = softmax(dot_nt(stacked(cq[own, cut]), ck[span_keys, cut]))
                lse[2, own, 2 * p : 2 * p + 1] = total[:SPAN]
                lse[2, own, 2 * p + 1 : 2 * p + 2] = total[SPAN:]
                parts.append(merged(dot(weights.astype(BF), cv[span_keys, cut])))
            outs.append(jnp.concatenate(parts, axis=1))
        os_[1] = shift_down(jnp.concatenate(outs, axis=0)).astype(BF)
        arrived((1, "out"))
        k = exchange_start(dot(os_[1], wo[1]))
        send_attended(1)
        return k

    def cross_backward():
        low = hbuf[...].astype(BF)
        send_upstream(1, low)
        dos[...] = shift_up(dot_nt(low, wo[1])).astype(BF)
        query_grads = []
        for c in range(spans):
            own = slice(c * SPAN, (c + 1) * SPAN)
            span_keys = slice(c * keys, (c + 1) * keys)
            parts = []
            for p in range(pairs):
                cut = slice(2 * HEAD_DIM * p, 2 * HEAD_DIM * (p + 1))
                q2 = stacked(cq[own, cut])
                do2 = stacked(dos[own, cut])
                scores = dot_nt(q2, ck[span_keys, cut])
                total = jnp.concatenate(
                    [lse[2, own, 2 * p : 2 * p + 1], lse[2, own, 2 * p + 1 : 2 * p + 2]], axis=0
                )
                weights = jnp.exp(scores - total)
                grads = dot_nt(do2, cv[span_keys, cut])
                inner = jnp.sum(weights * grads, axis=-1, keepdims=True)
                score_grad = (weights * (grads - inner)).astype(BF)
                parts.append(SCALE * merged(dot(score_grad, ck[span_keys, cut])))
                dkn[span_keys, cut] = dot_tn(score_grad, q2).astype(BF)
                dvn[span_keys, cut] = dot_tn(weights.astype(BF), do2).astype(BF)
            query_grads.append(jnp.concatenate(parts, axis=1))
        dqk[1, :, :width] = shift_down(jnp.concatenate(query_grads, axis=0)).astype(BF)
        send_grads(1)
        k = exchange_start(dot_nt(dqk[1, :, :width], unit(1, 0, 0, width)))

        sm[12:13, :] = column_sum(low)
        sm[20:21, :width] = column_sum(dqk[1, :, :width])
        sm[21:22, :width] = column_sum(dvn[...])
        norm_backward(1, exchange_wait(k))

    def neighbours_start():
        def feature_half(which):
            key_rows = units[1, 0, which, :, :, :, :, second].reshape(dim // 2, width)
            value_rows = units[1, 1, which, :, :, :, :, first].reshape(dim // 2, width)
            return dot_nt(dkn[...], key_rows) + dot_nt(dvn[...], value_rows)

        given = feature_half(1 - t).astype(BF)
        for q in range(ff // width):
            gp[1, :, q * width : (q + 1) * width] = given[q * rows : (q + 1) * rows]
        other = push(gp.at[1], gp.at[0], sib)
        nbr_sum[0] = (other, feature_half(t).astype(BF))

    def cross_key_weights():
        unit_store(1, 0, width, dot_tn(nsel[...], dkn[...]))
        factors["k"] = push(units.at[1, 0, :, :, :, 1 - x, :, second], rx0.at[0], px)

    def cross_value_weights():
        unit_store(1, 1, 0, dot_tn(nsel[...], dvn[...]))
        factors["v"] = push(units.at[1, 1, :, :, 1 - y, :, :, first], rx0.at[1], py)

    nbr_sum = [None]

    def neighbours_end():
        other, keep = nbr_sum[0]
        other.wait_recv()
        first_store = len(stores)
        taken = [gp[0, :, q * width : (q + 1) * width].astype(F32) for q in range(ff // width)]
        total = keep.astype(F32) + jnp.concatenate(taken, axis=0)
        for slot in range(pool):
            summed = jnp.zeros((length, total.shape[1]), F32)
            for pick in range(pool):
                hit = jnp.where(assign[pick % 2, pick // 2] == slot, F32(1.0), F32(0.0))
                summed += hit * total[pick * length : (pick + 1) * length]
            place = slot % nbr_o.shape[0]
            if slot >= nbr_o.shape[0]:
                stores[first_store + place].wait()
                stores[first_store + place] = None
            nbr_o[place] = summed
            store(nbr_o.at[place], nbr_h.at[slot])

    cuts = [slice(c * dim, (c + 1) * dim) for c in range(ff // dim)]

    def mlp_forward(j):
        arrived("mlp%d" % j)
        part = None
        for cut in cuts:
            pre = dot(ag[2 * j, 0], win[j, :, cut]) + in_b[j : j + 1, cut]
            active, slope = gelu_parts(pre)
            gp[j, :, cut] = slope.astype(BF)
            term = dot(active.astype(BF), wout[j, cut, :])
            part = term if part is None else part + term
        return exchange_start(part)

    def mlp_backward(j):
        low = ag[2 * j + 1, 0]
        sm[13 + j : 14 + j, :] = column_sum(low)
        part = None
        for c, cut in enumerate(cuts):
            down = dot_nt(low, wout[j, cut, :])
            pre_grad = (down * gp[j, :, cut].astype(F32)).astype(BF)
            sm[24 + 2 * j + c : 25 + 2 * j + c, :] = column_sum(pre_grad)
            term = dot_nt(pre_grad, win[j, :, cut])
            part = term if part is None else part + term
        k = exchange_start(part)
        return k

    def mlp_rows(j):
        gather_wait(2 * j)
        gather_wait(2 * j + 1)

        def bucket(b, carry):
            for c in range(2):
                turn(turned, ag[2 * j + c, b])
                part = turned[:, :, y, x] if j == 0 else turned[z1, z0]
                turned_rows[c, b] = part.reshape(4 * block, rows)
            return carry

        lax.fori_loop(0, 4, bucket, 0)

    def mlp_weights(j, c):
        cut = cuts[c]
        acc[...] = jnp.zeros_like(acc)

        def bucket(b, carry):
            pre = dot(ag[2 * j, b], win[j, :, cut]) + in_b[j : j + 1, cut]
            active, slope = gelu_parts(pre)
            pre_grad = (dot_nt(ag[2 * j + 1, b], wout[j, cut, :]) * slope).astype(BF)
            acc[0] += dot(turned_rows[0, b], pre_grad)
            acc[1] += dot(turned_rows[1, b], active.astype(BF))
            return carry

        lax.fori_loop(0, 4, bucket, 0)
        zst[j, c] = acc[...].astype(BF).reshape(2, 2, 2, block, dim)
        if j == 0:
            chain = Chain(lambda s: zst.at[0, c, :, s // 2, s % 2], rz.at[c])
            scatter["z", c] = chain
            chain.first()
        elif c == 0:
            scatter["w", c] = push(zst.at[1, c, :, :, 1 - x], rw0.at[c], px)
        else:
            scatter["w", c] = push(zst.at[1, c, :, 1 - y], rw0.at[c], py)

    def mlp_second(c):
        scatter["w", c].wait_recv()
        got = rw0[c].astype(F32)
        if c == 0:
            zst[1, c, :, :, x] = (zst[1, c, :, :, x].astype(F32) + got).astype(BF)
            scatter["w", c] = push(zst.at[1, c, :, 1 - y, x], rw1.at[c], py)
        else:
            zst[1, c, :, y] = (zst[1, c, :, y].astype(F32) + got).astype(BF)
            scatter["w", c] = push(zst.at[1, c, :, y, 1 - x], rw1.at[c], px)

    def mlp_end(j, c):
        if j == 0:
            scatter["z", c].end(gm_o.at[j, c])
        else:
            scatter["w", c].wait_recv()
            gm_o[j, c] = zst[1, c, :, y, x].astype(F32) + rw1[c].astype(F32)
        store(gm_o.at[j, c], gm_h.at[j, :, :, pl.ds(c * dim, dim)])

    live = lax.broadcasted_iota(jnp.int32, (rows, dim), 0) < lengths[0]
    sm[...] = jnp.zeros_like(sm)
    arrived("hidden")
    hbuf[...] = dqk[0].astype(F32)
    norm_forward(0, into_us(0))
    arrived("cot")
    ag[3, 0] = jnp.where(live, ag[3, 0], jnp.zeros((rows, dim), BF))
    entered()
    gather_start(3, (pz0, pz1, pz))
    send_inputs(0)
    k = self_forward(0)
    cross_keys()
    hbuf[...] += exchange_wait(k) + sa_ob[0:1, :]
    norm_forward(1, into_us(1))
    k = cross_forward()
    send_inputs(1)
    hbuf[...] += exchange_wait(k) + ca_ob[...].reshape(1, dim)
    norm_forward(2, into_ag(0))
    gather_start(0)
    k = mlp_forward(0)
    hbuf[...] += exchange_wait(k) + out_b[0:1, :]
    norm_forward(3, into_us(2))
    k = self_forward(1)
    send_inputs(2)
    hbuf[...] += exchange_wait(k) + sa_ob[1:2, :]
    norm_forward(4, into_ag(2))
    gather_start(2, (pz0, pz1, pz))
    k = mlp_forward(1)
    gather_forward(0)
    final = hbuf[...] + exchange_wait(k) + out_b[1:2, :]
    hid_o[...] = jnp.where(live, final, 0.0).astype(BF)
    store(hid_o, hid_h)
    hbuf[...] = ag[3, 0].astype(F32)

    small_copy = []
    small_bufs = [sm] + [small_o.at[q] for q in range(4)]

    def small_step(k):
        if k:
            small_copy[-1].wait_recv()
            small_bufs[k][...] = small_bufs[k - 1][...] + rsm[k - 1]
        if k < 4:
            small_copy.append(push(small_bufs[k], rsm.at[k], (px, py, pz0, pz1)[k]))
        else:
            store(small_o.at[3], small_h)

    def feed_back(j):
        norm_backward(4 if j else 2, exchange_wait(mlp_backward(j)))

    def first_grads():
        ag[1, 0] = hbuf[...].astype(BF)
        gather_start(1, (px, py, pxy))

    def last_attention():
        self_backward(0)
        store(hbuf, grad_h)

    steps = {
        "b1": lambda: feed_back(1),
        "b0": lambda: feed_back(0),
        "S2": lambda: self_backward(1),
        "S0": last_attention,
        "d1": first_grads,
        "g2": lambda: send_grads(2),
        "C": cross_backward,
        "Cn": neighbours_start,
        "Ck": cross_key_weights,
        "Cv": cross_value_weights,
        "gswd2": lambda: gather_swap(3),
        "gswd1": lambda: gather_swap(1),
        "gswu2": lambda: gather_swap(2),
        "gru1": lambda: gather_relay(0),
        "rows0": lambda: mlp_rows(0),
        "rows1": lambda: mlp_rows(1),
        "nbr": neighbours_end,
    }
    for n in range(5):
        steps["sm%d" % n] = partial(small_step, n)
    for n in range(2):
        steps["mw0%d" % n] = partial(mlp_weights, 0, n)
        steps["mw1%d" % n] = partial(mlp_weights, 1, n)
        steps["mz2%d" % n] = lambda n=n: scatter["z", n].second()
        steps["mz3%d" % n] = lambda n=n: scatter["z", n].third()
        steps["mze%d" % n] = partial(mlp_end, 0, n)
        steps["ms%d" % n] = partial(mlp_second, n)
        steps["me%d" % n] = partial(mlp_end, 1, n)
    for layer in range(3):
        steps["rf%d" % layer] = partial(relay_factors, layer)
        for n in range(2):
            steps["s1%s%d" % ("ab"[n], layer)] = partial(scatter_one, layer, n)
            steps["s2%d%d" % (layer, n)] = partial(scatter_two, layer, n)
            steps["s3%d%d" % (layer, n)] = partial(scatter_three, layer, n)
            steps["s4%d%d" % (layer, n)] = partial(scatter_four, layer, n)
            steps["se%d%d" % (layer, n)] = partial(scatter_end, layer, n)
    for name in ORDER:
        steps[name]()
    for copy in stores:
        if copy is not None:
            copy.wait()
    for copy in sends:
        copy.wait_send()
    for chain in chains:
        chain.sent()
    for k in (ex[0] - 2, ex[0] - 1):
        ex_copy[k].wait_send()


def finish(hid, grad, nbr, ga, gm, small, *refs):
    (
        hid_o, grad_o, nbr_o, gain_o, bias_o, sa_qkv_o, sa_b_o, sa_out_o, sa_ob_o, ca_qkv_o,
        ca_b_o, ca_out_o, ca_ob_o, in_o, in_b_o, out_o, out_b_o,
        hid_v, grad_v, nbr_v, ga_v, gm_v, get, put,
    ) = refs
    width = ca_out_o.shape[1]
    dim = gain_o.shape[1]

    def fetch(k, src, dst):
        copy = pltpu.make_async_copy(src, dst, get.at[k])
        copy.start()
        return copy

    fetched = [
        fetch(k, src, dst)
        for k, (src, dst) in enumerate(
            ((nbr, nbr_v), (gm, gm_v), (ga, ga_v), (grad, grad_v), (hid, hid_v))
        )
    ]
    copies = []

    def move(src, dst):
        copy = pltpu.make_async_copy(src, dst, put.at[len(copies)])
        copy.start()
        copies.append(copy)

    gain_o[...] = small[0:5, :]
    bias_o[...] = small[5:10, :]
    sa_ob_o[...] = small[10:12, :]
    ca_ob_o[...] = small[12, :]
    out_b_o[...] = small[13:15, :]
    for j in range(2):
        sa_b_o[j] = small[16 + 2 * j : 18 + 2 * j, :width]
    ca_b_o[...] = small[20:22, :width]
    for j in range(2):
        for c in range(in_b_o.shape[1] // dim):
            in_b_o[j : j + 1, c * dim : (c + 1) * dim] = small[24 + 2 * j + c : 25 + 2 * j + c, :]
    fetched[0].wait()
    move(nbr_v, nbr_o)
    fetched[1].wait()
    for j in range(2):
        move(gm_v.at[j, 0], in_o.at[j])
        move(gm_v.at[j, 1], out_o.at[j])
    fetched[2].wait()
    for a, out, rows in (
        (0, sa_qkv_o.at[0], sa_out_o.at[0]), (1, ca_qkv_o, ca_out_o),
        (2, sa_qkv_o.at[1], sa_out_o.at[1]),
    ):
        move(ga_v.at[a, 0, :, pl.ds(0, width)], out.at[0])
        move(ga_v.at[a, 0, :, pl.ds(width, width)], out.at[1])
        move(ga_v.at[a, 1, :, pl.ds(0, width)], out.at[2])
        move(ga_v.at[a, 1, :, pl.ds(width, width)], rows)
    fetched[3].wait()
    move(grad_v, grad_o)
    fetched[4].wait()
    move(hid_v, hid_o)
    for copy in copies:
        copy.wait()


def on_device(
    n_dp,
    hidden_in, lengths, neighbours, assign, cotangent, norm_gain, norm_bias, sa_qkv, sa_bias,
    sa_out, sa_out_bias, ca_qkv, ca_bias, ca_out, ca_out_bias, mlp_in, mlp_in_bias, mlp_out,
    mlp_out_bias,
):
    rows, dim = hidden_in.shape
    width = sa_out.shape[1]
    ff = mlp_in.shape[2]
    pool, length = neighbours.shape[0], neighbours.shape[1]
    block = dim // GROUPS
    picks = assign.size * length
    vmem = pl.BlockSpec(memory_space=pltpu.VMEM)
    smem = pl.BlockSpec(memory_space=pltpu.SMEM)
    hbm = pl.BlockSpec(memory_space=pl.ANY)

    def array(*shape, dtype=F32):
        return jax.ShapeDtypeStruct(shape, dtype)

    outs = (
        array(rows, dim, dtype=BF),
        array(rows, dim),
        array(pool, length, width),
        array(3, 2, block, 2 * width),
        array(2, 2, block, ff),
        array(SMALL_ROWS, dim),
    )
    V = pltpu.VMEM
    scratch = [
        V((rows, dim), BF),
        V((pool // 2, length, width), F32),
        V((3, 2, block, 2 * width), F32),
        V((2, ff // dim, 2, block, dim), F32),
        V((4, SMALL_ROWS, dim), F32),
        V((3, 2, 2, 2, 2, 2, block, 2 * width), BF),
        V((3, width, dim), BF),
        V((2, dim, ff), BF),
        V((2, ff, dim), BF),
        V((picks, dim), BF),
        V((4, 4, rows, dim), BF),
        V((3, rows, dim), BF),
        V((5, rows, dim), BF),
        V((5, rows, 1), F32),
        V((2, rows, width), BF),
        V((2, rows, width), BF),
        V((2, rows, width), BF),
        V((3, rows, width), BF),
        V((rows, width), BF),
        V((picks, width), BF),
        V((picks, width), BF),
        V((3, rows, 128), F32),
        V((2, rows, ff), BF),
        V((3, rows, 2 * width), BF),
        V((2, rows, width), BF),
        V((picks, width), BF),
        V((picks, width), BF),
        V((rows, width), BF),
        V((2, rows, dim), BF),
        V((2, rows, dim), BF),
        V((2, 2, 2, 2, block, width), BF),
        V((3, 2, 2, 2, block, 2 * width), BF),
        V((3, 2, 5, block, 2 * width), BF),
        V((2, 4 * block, dim), F32),
        V((2, ff // dim, 2, 2, 2, block, dim), BF),
        V((ff // dim, 5, 2, block, dim), BF),
        V((ff // dim, 2, 2, block, dim), BF),
        V((ff // dim, 2, block, dim), BF),
        V((SMALL_ROWS, dim), F32),
        V((4, SMALL_ROWS, dim), F32),
        V((rows, dim), F32),
        V((3, 2, 2, 2, 2, block, rows), BF),
        V((3, 2, 2, 2, 2, block, rows), BF),
        V((3, 2, 2, 2, block, rows), BF),
        V((2, 2, 2, 2, block, rows), BF),
        V((3, 2, 2, 2, block, rows), BF),
        V((3, rows, width), BF),
        V((3, rows, 2 * width), BF),
        V((2, rows, width), BF),
        V((2, 2, 2, 2, block, rows), BF),
        V((2, 4, 4 * block, rows), BF),
        pltpu.SemaphoreType.DMA((64,)),
        pltpu.SemaphoreType.DMA((160,)),
        pltpu.SemaphoreType.DMA((160,)),
    ]
    hid, grad, nbr, ga, gm, small = pl.pallas_call(
        partial(kernel, n_dp),
        out_shape=outs,
        in_specs=[smem] * 2 + [vmem] * 8 + [hbm] * 9,
        out_specs=(hbm,) * 6,
        scratch_shapes=scratch,
        compiler_params=pltpu.CompilerParams(
            collective_id=0, has_side_effects=True, vmem_limit_bytes=64 * 1024 * 1024 - 65536
        ),
    )(
        lengths, assign.T, norm_gain, norm_bias, sa_bias, sa_out_bias,
        ca_bias, ca_out_bias, mlp_in_bias, mlp_out_bias,
        hidden_in, cotangent, neighbours, sa_qkv, sa_out, ca_qkv, ca_out, mlp_in, mlp_out,
    )
    rest = n_dp // GROUPS
    if rest > 1:
        members = [[a * rest + b for b in range(rest)] for a in range(GROUPS)]
        ga = lax.psum_scatter(ga, "dp", scatter_dimension=2, axis_index_groups=members, tiled=True)
        gm = lax.psum_scatter(gm, "dp", scatter_dimension=2, axis_index_groups=members, tiled=True)
        small = lax.psum(small, "dp", axis_index_groups=members)
    owned = block // rest
    results = pl.pallas_call(
        finish,
        out_shape=(
            outs[0],
            outs[1],
            outs[2],
            array(5, dim),
            array(5, dim),
            array(2, 3, owned, width),
            array(2, 2, width),
            array(2, owned, width),
            array(2, dim),
            array(3, owned, width),
            array(2, width),
            array(owned, width),
            array(dim),
            array(2, owned, ff),
            array(2, ff),
            array(2, owned, ff),
            array(2, dim),
        ),
        in_specs=[hbm] * 5 + [vmem],
        out_specs=tuple(
            hbm if k in (0, 1, 2, 5, 7, 9, 11, 13, 15) else vmem for k in range(17)
        ),
        scratch_shapes=[
            V((rows, dim), BF),
            V((rows, dim), F32),
            V((pool, length, width), F32),
            V((3, 2, owned, 2 * width), F32),
            V((2, 2, owned, ff), F32),
            pltpu.SemaphoreType.DMA((8,)),
            pltpu.SemaphoreType.DMA((32,)),
        ],
    )(hid, grad, nbr, ga, gm, small)
    results = list(results)
    for k in (7, 11, 15):
        results[k] = results[k].swapaxes(-1, -2)
    return tuple(results)


def solution(mesh):
    return jax.shard_map(
        partial(on_device, mesh.shape["dp"]),
        mesh=mesh,
        in_specs=(
            P("dp", None),
            P("dp"),
            P("dp", None, None),
            P("dp", None),
            P("dp", None),
            P(),
            P(),
            P(None, None, None, "tensor"),
            P(None, None, "tensor"),
            P(None, "tensor", None),
            P(),
            P(None, None, "tensor"),
            P(None, "tensor"),
            P("tensor", None),
            P(),
            P(None, None, "tensor"),
            P(None, "tensor"),
            P(None, "tensor", None),
            P(),
        ),
        out_specs=(
            P("dp", None),
            P("dp", None),
            P("dp", None, "tensor"),
            P(),
            P(),
            P(None, None, "dp", "tensor"),
            P(None, None, "tensor"),
            P(None, "tensor", "dp"),
            P(),
            P(None, "dp", "tensor"),
            P(None, "tensor"),
            P("tensor", "dp"),
            P(),
            P(None, "dp", "tensor"),
            P(None, "tensor"),
            P(None, "tensor", "dp"),
            P(),
        ),
        check_vma=False,
    )
```

```python
from functools import partial

import jax
import jax.numpy as jnp
from jax import lax
from jax.experimental import pallas as pl
from jax.experimental.pallas import tpu as pltpu
from jax.sharding import PartitionSpec as P

HEAD_DIM = 64
SPAN = 64
GROUPS = 16
EPSILON = 1e-05
SCALE = 0.125
MASKED = -1e30
MESH = pl.DeviceIdType.MESH
BF = jnp.bfloat16
F32 = jnp.float32
SMALL_ROWS = 32
ORDER = (
    "b1", "S2a", "S2b", "d1", "b0a", "gswd2", "b0b", "g2", "Ca", "gru1", "Cn", "gswd1", "Cv", "Ck",
    "rows0", "rf2", "mw01", "rf1", "s1a2", "mw00", "Cb", "S0a", "mz21", "gswu2", "rf0", "S0b",
    "s1b2", "s1b0", "s1a1", "s220", "sm0", "s1a0", "mz20", "rows1", "s1b1", "s221", "s320", "mw11",
    "s201", "s321", "mz31", "s420", "mz30", "mw10", "s210", "s200", "s301", "nbr", "s310", "s211",
    "s421", "sm1", "s300", "ms1", "s410", "s401", "ms0", "mze0", "sm2", "s311", "s400", "sm3",
    "se01", "mze1", "se21", "s411", "me1", "se10", "se00", "se20", "sm4", "me0", "se11",
)


def dot(a, b):
    return jnp.dot(a, b, preferred_element_type=F32)


def dot_nt(a, b):
    return lax.dot_general(a, b, (((1,), (1,)), ((), ())), preferred_element_type=F32)


def dot_tn(a, b):
    return lax.dot_general(a, b, (((0,), (0,)), ((), ())), preferred_element_type=F32)


def column_sum(values):
    return jnp.sum(values.astype(F32), axis=0, keepdims=True)


def gelu_parts(a):
    phi = 0.5 * (1.0 + lax.erf(a * 0.7071067811865476))
    density = 0.3989422804014327 * jnp.exp(-0.5 * a * a)
    return a * phi, phi + a * density


def kernel(n_dp, *refs):
    (
        lengths, assign, gain, bias, sa_b, sa_ob, ca_b, ca_ob, in_b, out_b,
        hidden, cot, n_ref, w_sa_qkv, w_sa_out, w_ca_qkv, w_ca_out, w_in, w_out,
        hid_h, grad_h, nbr_h, ga_h, gm_h, gain_h, bias_h, sa_ob_h, ca_ob_h, out_b_h, sa_b_h, ca_b_h,
        in_b_h,
        hid_o, nbr_o, ga_o, gm_o, small_o, gain_o, bias_o, sa_ob_o, ca_ob_o, out_b_o, sa_b_o, ca_b_o,
        in_b_o,
        units, wo, win, wout, nsel, ag, us, xh, rstd, qs, ks, vs, os_, cq, ck, cv,
        lse, gp, dqk, dvs, dkn, dvn, dos, xs, xr, rx0, rx1, rx2,
        acc, zst, rz, rw0, rw1, sm, rsm, hbuf,
        ut, dt, rut_x, rut_y, rdt, ro, rdqk, rdv, turned, turned_rows,
        lsem, ssem, rsem,
    ) = refs
    rows, dim = hbuf.shape
    width = wo.shape[1]
    ff = win.shape[2]
    block = dim // GROUPS
    half = rows // 2
    i = lax.axis_index("dp")
    t = lax.axis_index("tensor")
    m = n_dp // GROUPS
    g = i // m
    r = i % m
    x = g % 2
    y = (g // 2) % 2
    z0 = (g // 4) % 2
    z1 = g // 8
    px = ((g + 1 - 2 * x) * m + r, t)
    py = ((g + 2 - 4 * y) * m + r, t)
    pxy = ((g + 3 - 2 * x - 4 * y) * m + r, t)
    pz0 = ((g + 4 - 8 * z0) * m + r, t)
    pz1 = ((g + 8 - 16 * z1) * m + r, t)
    pz = ((g + 12 - 8 * z0 - 16 * z1) * m + r, t)
    zz = g // 4
    sib = (i, 1 - t)
    count = [0, 0]
    sends = []

    def load(src, dst):
        copy = pltpu.make_async_copy(src, dst, lsem.at[count[0]])
        count[0] += 1
        copy.start()
        return copy

    stores = []

    def store(src, dst):
        stores.append(load(src, dst))

    def push(src, dst, to):
        k = count[1]
        count[1] += 1
        copy = pltpu.make_async_remote_copy(
            src_ref=src, dst_ref=dst, send_sem=ssem.at[k], recv_sem=rsem.at[k],
            device_id=to, device_id_type=MESH,
        )
        copy.start()
        sends.append(copy)
        return copy

    loads = {}

    def load_attention(layer, src):
        def blocks(c):
            return src(c).reshape(2, 2, 2, 2, block, width)

        loads[layer, "qkv"] = [
            load(blocks(0), units.at[layer, 0, :, :, :, :, :, pl.ds(0, width)]),
            load(blocks(1), units.at[layer, 0, :, :, :, :, :, pl.ds(width, width)]),
            load(blocks(2), units.at[layer, 1, :, :, :, :, :, pl.ds(0, width)]),
        ]

    load_attention(0, lambda c: w_sa_qkv.at[0, c])
    loads[0, "out"] = [load(w_sa_out.at[0], wo.at[0])]
    loads["cot"] = [load(cot, ag.at[3, 0])]
    load_attention(1, lambda c: w_ca_qkv.at[c])
    pool, length = n_ref.shape[0], n_ref.shape[1]
    loads["n"] = [
        load(n_ref.at[:, :, pl.ds(c * width, width)], into.reshape(pool, length, width))
        for c, into in enumerate((dkn, dvn))
    ]
    loads[1, "out"] = [load(w_ca_out, wo.at[1])]
    loads["mlp0"] = [load(w_in.at[0], win.at[0]), load(w_out.at[0], wout.at[0])]
    load_attention(2, lambda c: w_sa_qkv.at[1, c])
    loads[2, "out"] = [load(w_sa_out.at[1], wo.at[2])]
    loads["mlp1"] = [load(w_in.at[1], win.at[1]), load(w_out.at[1], wout.at[1])]

    def arrived(key):
        for copy in loads[key]:
            copy.wait()

    barrier = pltpu.get_barrier_semaphore()
    partners = (sib, px, py, pxy, pz0, pz1, pz)
    for to in partners:
        pl.semaphore_signal(barrier, inc=1, device_id=to, device_id_type=MESH)

    def entered():
        pl.semaphore_wait(barrier, len(partners))

    def unit(layer, which, first, size):
        value = units[layer, which, :, :, :, :, :, pl.ds(first, size)]
        return value.reshape(dim, size)

    def unit_store(layer, which, first, value):
        size = value.shape[1]
        units[layer, which, :, :, :, :, :, pl.ds(first, size)] = value.astype(BF).reshape(
            2, 2, 2, 2, block, size
        )

    ex = [0]
    ex_copy = {}

    pieces = (pl.ds(0, 2 * dim // 3), pl.ds(2 * dim // 3, dim // 3))

    def exchange_start(part):
        k = ex[0]
        ex[0] += 1
        slot = k % 2
        ex_copy[k] = []
        for c, columns in enumerate(pieces):
            if k >= 2:
                ex_copy[k - 2][c].wait_send()
            xs[slot, :, columns] = part(c).astype(BF)
            copy = pltpu.make_async_remote_copy(
                src_ref=xs.at[slot, :, columns], dst_ref=xr.at[slot, :, columns],
                send_sem=ssem.at[156 + 2 * slot + c], recv_sem=rsem.at[156 + 2 * slot + c],
                device_id=sib, device_id_type=MESH,
            )
            copy.start()
            ex_copy[k].append(copy)
        return k

    def whole(part):
        return lambda c: part[:, pieces[c].start : pieces[c].start + pieces[c].size]

    def exchange_wait(k):
        for copy in ex_copy[k]:
            copy.wait_recv()
        return xs[k % 2].astype(F32) + xr[k % 2].astype(F32)

    gathers = {}

    mine = pl.ds(pl.multiple_of(t * half, half), half)
    quarter = half // 2
    upper = pl.ds(pl.multiple_of(t * half, quarter), quarter)
    lower = pl.ds(pl.multiple_of(t * half + quarter, quarter), quarter)

    def gather_start(a, peers=(px, py)):
        gathers[a] = [
            push(ag.at[a, 0, mine], ag.at[a, p + 1, mine], to) for p, to in enumerate(peers)
        ]

    def gather_swap(a):
        for copy in gathers[a]:
            copy.wait_recv()
        gathers[a] = [push(ag.at[a, p, mine], ag.at[a, p, mine], sib) for p in (1, 2, 3)]

    def gather_forward(a):
        for copy in gathers[a]:
            copy.wait_recv()
        gathers[a] = [
            push(ag.at[a, 1, upper], ag.at[a, 3, upper], py),
            push(ag.at[a, 2, lower], ag.at[a, 3, lower], px),
        ] + [push(ag.at[a, p, mine], ag.at[a, p, mine], sib) for p in (1, 2)]

    def gather_relay(a):
        for copy in gathers[a][:2]:
            copy.wait_recv()
        gathers[a] = gathers[a][2:] + [push(ag.at[a, 3, mine], ag.at[a, 3, mine], sib)]

    def gather_wait(a):
        for copy in gathers[a]:
            copy.wait_recv()

    UP, DOWN = {1: 0, 2: 1, 3: 2}, {0: 3, 1: 4, 2: 0}
    above = ((g + 4) * m + r, t)
    below = ((g - 4) * m + r, t)
    chains = []

    class Chain:
        def __init__(self, shard, into):
            self.base = count[1]
            count[1] += 5
            self.shard, self.into = shard, into
            chains.append(self)

        def copy(self, s, slot, to):
            return pltpu.make_async_remote_copy(
                src_ref=self.shard(s), dst_ref=self.into.at[slot],
                send_sem=ssem.at[self.base + slot], recv_sem=rsem.at[self.base + slot],
                device_id=to, device_id_type=MESH,
            )

        def arrive(self, s, slot):
            self.copy(s, slot, above).wait_recv()
            return self.into[slot].astype(F32)

        def pass_on(self, s, slot, to):
            own = self.shard(s)
            own[...] = (own[...].astype(F32) + self.arrive(s, slot)).astype(BF)
            self.copy(s, slot, to).start()

        def first(self):
            @pl.when(zz == 0)
            def _():
                for s in (3, 2, 1):
                    self.copy(s, UP[s], above).start()

            @pl.when(zz == 3)
            def _():
                for s in (0, 1, 2):
                    self.copy(s, DOWN[s], below).start()

        def second(self):
            @pl.when(zz == 1)
            def _():
                for s in (3, 2):
                    self.pass_on(s, UP[s], above)

            @pl.when(zz == 2)
            def _():
                for s in (0, 1):
                    self.pass_on(s, DOWN[s], below)

        def third(self):
            @pl.when(zz == 2)
            def _():
                self.pass_on(3, UP[3], above)

            @pl.when(zz == 1)
            def _():
                self.pass_on(0, DOWN[0], below)

        def end(self, out):
            for s in range(4):
                @pl.when(zz == s)
                def _(s=s):
                    total = self.shard(s)[...].astype(F32)
                    if s > 0:
                        total += self.arrive(s, UP[s])
                    if s < 3:
                        total += self.arrive(s, DOWN[s])
                    out[...] = total

        def sent(self):
            for z, slots in enumerate(
                ((UP[1], UP[2], UP[3]), (UP[2], UP[3], DOWN[0]),
                 (UP[3], DOWN[0], DOWN[1]), (DOWN[0], DOWN[1], DOWN[2]))
            ):
                @pl.when(zz == z)
                def _(slots=slots):
                    for slot in slots:
                        self.copy(0, slot, above).wait_send()

    def turn(dst, value):
        dst[...] = value.T.reshape(2, 2, 2, 2, block, rows)

    scatter = {}
    factors = {}

    bits, partner = (x, y), (px, py)

    def axis_of(layer, which):
        return 1 - which if layer == 0 else which

    def half_at(a, v):
        return (slice(None),) * (3 - a) + (v,)

    def quarter_at(a, v, w):
        return (slice(None), slice(None)) + ((w, v) if a == 0 else (v, w))

    def send_inputs(layer):
        turn(ut.at[layer], us[layer])
        for name, which, into in (("u0", 0, rut_x), ("u1", 1, rut_y)):
            if name == "u1" and layer == 1:
                continue
            a = axis_of(layer, which)
            place = layer if which == 0 else layer // 2
            factors[layer, name] = push(
                ut.at[(layer, t) + half_at(a, 1 - bits[a])[1:]], into.at[place, t], partner[a]
            )

    def send_attended(layer):
        factors[layer, "o"] = push(os_.at[layer], ro.at[layer], partner[axis_of(layer, 1)])

    def send_upstream(layer, low):
        turn(dt.at[layer], low)
        a = axis_of(layer, 1)
        factors[layer, "d"] = push(
            dt.at[(layer, t) + half_at(a, 1 - bits[a])[1:]], rdt.at[layer, t], partner[a]
        )

    def relay_factor(layer, name):
        into = {"u0": rut_x.at[layer, t], "u1": rut_y.at[layer // 2, t], "d": rdt.at[layer, t]}
        factors[layer, name].wait_recv()
        factors[layer, name] = push(into[name], into[name], sib)

    def relay_factors(layer):
        relay_factor(layer, "u0")
        if layer != 1:
            relay_factor(layer, "u1")
        relay_factor(layer, "d")

    def send_grads(layer):
        to = partner[axis_of(layer, 0)]
        if layer == 1:
            factors[layer, "0"] = push(
                dqk.at[layer, :, pl.ds(0, width)], rdqk.at[layer, :, pl.ds(0, width)], to
            )
        else:
            factors[layer, "0"] = push(dqk.at[layer], rdqk.at[layer], to)
            factors[layer, "1"] = push(
                dvs.at[layer // 2], rdv.at[layer // 2], partner[axis_of(layer, 1)]
            )

    first, second = pl.ds(0, width), pl.ds(width, width)

    def scatter_one(layer, which):
        a = axis_of(layer, which)
        mine_at = half_at(a, bits[a])
        unit_at = (layer, which) + mine_at + (slice(None),) * a

        def put(columns, total):
            units[unit_at + (slice(None), columns)] = total.astype(BF).reshape(
                2, 2, 2, block, total.shape[1]
            )

        def rows_of(ref):
            return ref[(layer,) + mine_at].reshape(dim // 2, rows)

        def add(name, columns):
            factors[name].wait_recv()
            at = unit_at + (slice(None), columns)
            units[at] = (units[at].astype(F32) + rx0[which].astype(F32)).astype(BF)

        if which == 0:
            for name in ("u0", "0"):
                factors[layer, name].wait_recv()
            size = width if layer == 1 else 2 * width
            put(
                pl.ds(0, size),
                dot(rows_of(ut), dqk[layer, :, :size])
                + dot(rut_x[layer].reshape(dim // 2, rows), rdqk[layer, :, :size]),
            )
            if layer == 1:
                add("k", second)
        else:
            if layer == 1:
                add("v", first)
            else:
                for name in ("u1", "1"):
                    factors[layer, name].wait_recv()
                put(
                    first,
                    dot(rows_of(ut), dvs[layer // 2])
                    + dot(rut_y[layer // 2].reshape(dim // 2, rows), rdv[layer // 2]),
                )
            for name in ("o", "d"):
                factors[layer, name].wait_recv()
            put(
                second,
                dot(rows_of(dt), os_[layer])
                + dot(rdt[layer].reshape(dim // 2, rows), ro[layer]),
            )
        scatter[layer, which] = push(
            units.at[(layer, which) + quarter_at(a, bits[a], 1 - bits[1 - a])],
            rx1.at[layer, which], partner[1 - a],
        )

    def scatter_two(layer, which):
        scatter[layer, which].wait_recv()
        units[layer, which, :, :, y, x] = (
            units[layer, which, :, :, y, x].astype(F32) + rx1[layer, which].astype(F32)
        ).astype(BF)
        chain = Chain(
            lambda s: units.at[layer, which, s // 2, s % 2, y, x], rx2.at[layer, which]
        )
        scatter[layer, which] = chain
        chain.first()

    def scatter_three(layer, which):
        scatter[layer, which].second()

    def scatter_four(layer, which):
        scatter[layer, which].third()

    def scatter_end(layer, which):
        scatter[layer, which].end(ga_o.at[layer, which])
        store(ga_o.at[layer, which], ga_h.at[layer, which])

    def norm_forward(k, store):
        h = hbuf[...]
        centred = h - jnp.mean(h, axis=-1, keepdims=True)
        rec = lax.rsqrt(jnp.mean(centred * centred, axis=-1, keepdims=True) + EPSILON)
        normed = centred * rec
        xh[k] = normed.astype(BF)
        rstd[:, k : k + 1] = rec
        store((normed * gain[k : k + 1, :] + bias[k : k + 1, :]).astype(BF))

    def norm_backward(k, dy):
        normed = xh[k].astype(F32)
        sm[k : k + 1, :] = jnp.sum(dy * normed, axis=0, keepdims=True)
        sm[5 + k : 6 + k, :] = jnp.sum(dy, axis=0, keepdims=True)
        scaled = dy * gain[k : k + 1, :]
        first = jnp.mean(scaled, axis=-1, keepdims=True)
        second = jnp.mean(scaled * normed, axis=-1, keepdims=True)
        hbuf[...] += rstd[:, k : k + 1] * (scaled - first - normed * second)

    def into_us(k):
        def store(value):
            us[k] = value

        return store

    def into_ag(a):
        def store(value):
            ag[a, 0] = value

        return store

    def stacked(pair):
        lane = lax.broadcasted_iota(jnp.int32, pair.shape, 1)
        zero = jnp.zeros_like(pair)
        return jnp.concatenate(
            [jnp.where(lane < HEAD_DIM, pair, zero), jnp.where(lane < HEAD_DIM, zero, pair)],
            axis=0,
        )

    def merged(both_heads):
        count_rows = both_heads.shape[0] // 2
        lane = lax.broadcasted_iota(jnp.int32, (count_rows, both_heads.shape[1]), 1)
        return jnp.where(lane < HEAD_DIM, both_heads[:count_rows], both_heads[count_rows:])

    pairs = width // (2 * HEAD_DIM)

    def softmax(scores):
        top = jnp.max(scores, axis=-1, keepdims=True)
        terms = jnp.exp(scores - top)
        total = jnp.sum(terms, axis=-1, keepdims=True)
        return terms / total, top + jnp.log(total)

    def causal(scores):
        row_ids = lax.broadcasted_iota(jnp.int32, (rows, rows), 0)
        col_ids = lax.broadcasted_iota(jnp.int32, (rows, rows), 1)
        keep = col_ids <= row_ids
        return jnp.where(jnp.concatenate([keep, keep], axis=0), scores, MASKED)

    def self_forward(j):
        layer = 2 * j
        arrived((layer, "qkv"))
        u = us[layer]
        qk = dot(u, unit(layer, 0, 0, 2 * width))
        qs[j] = (qk[:, :width] + sa_b[j, 0:1, :]).astype(BF) * BF(SCALE)
        ks[j] = qk[:, width:].astype(BF)
        vs[j] = (dot(u, unit(layer, 1, 0, width)) + sa_b[j, 1:2, :]).astype(BF)
        for p in range(pairs):
            cut = slice(2 * HEAD_DIM * p, 2 * HEAD_DIM * (p + 1))
            weights, total = softmax(causal(dot_nt(stacked(qs[j, :, cut]), ks[j, :, cut])))
            lse[j, :, 2 * p : 2 * p + 1] = total[:rows]
            lse[j, :, 2 * p + 1 : 2 * p + 2] = total[rows:]
            os_[layer, :, cut] = merged(dot(weights.astype(BF), vs[j, :, cut])).astype(BF)
        arrived((layer, "out"))
        if j == 0:
            entered()
        k = exchange_start(lambda c: dot(os_[layer], wo[layer, :, pieces[c]]))
        send_attended(layer)
        return k

    def self_backward(j):
        layer = 2 * j
        low = hbuf[...].astype(BF)
        send_upstream(layer, low)
        dos[...] = dot_nt(low, wo[layer]).astype(BF)
        for p in range(pairs):
            cut = slice(2 * HEAD_DIM * p, 2 * HEAD_DIM * (p + 1))
            q2 = stacked(qs[j, :, cut])
            do2 = stacked(dos[:, cut])
            scores = causal(dot_nt(q2, ks[j, :, cut]))
            total = jnp.concatenate(
                [lse[j, :, 2 * p : 2 * p + 1], lse[j, :, 2 * p + 1 : 2 * p + 2]], axis=0
            )
            weights = jnp.exp(scores - total)
            grads = dot_nt(do2, vs[j, :, cut])
            inner = jnp.sum(weights * grads, axis=-1, keepdims=True)
            score_grad = (weights * (grads - inner)).astype(BF)
            dqk[layer, :, cut] = (SCALE * merged(dot(score_grad, ks[j, :, cut]))).astype(BF)
            dqk[layer, :, slice(width + cut.start, width + cut.stop)] = dot_tn(
                score_grad, q2
            ).astype(BF)
            dvs[j, :, cut] = dot_tn(weights.astype(BF), do2).astype(BF)
        if j == 0:
            send_grads(layer)
        k = exchange_start(
            whole(
                dot_nt(dqk[layer], unit(layer, 0, 0, 2 * width))
                + dot_nt(dvs[j], unit(layer, 1, 0, width))
            )
        )
        sm[10 + j : 11 + j, :] = column_sum(low)
        sm[16 + 2 * j : 17 + 2 * j, :width] = column_sum(dqk[layer, :, :width])
        sm[17 + 2 * j : 18 + 2 * j, :width] = column_sum(dvs[j])
        return k

    spans = rows // SPAN
    keys = nsel.shape[0] // spans

    def shift_up(values):
        moved = pltpu.roll(values, rows - (SPAN - 1), 0)
        row_ids = lax.broadcasted_iota(jnp.int32, values.shape, 0)
        return jnp.where(row_ids < rows - (SPAN - 1), moved, 0.0)

    def shift_down(values):
        moved = pltpu.roll(values, SPAN - 1, 0)
        row_ids = lax.broadcasted_iota(jnp.int32, values.shape, 0)
        return jnp.where(row_ids >= SPAN - 1, moved, 0.0)

    def cross_keys():
        arrived((1, "qkv"))
        arrived("n")
        for pick in range(pool):
            own = slice(pick * length, (pick + 1) * length)
            rows_of = pl.ds(assign[pick % 2, pick // 2] * length, length)
            nsel[own, :width] = dkn[rows_of, :]
            nsel[own, width:] = dvn[rows_of, :]
        ck[...] = dot(nsel[...], unit(1, 0, width, width)).astype(BF)
        cv[...] = (dot(nsel[...], unit(1, 1, 0, width)) + ca_b[1:2, :]).astype(BF)

    def cross_forward():
        q = dot(us[1], unit(1, 0, 0, width)) + ca_b[0:1, :]
        cq[...] = shift_up(q).astype(BF) * BF(SCALE)
        outs = []
        for c in range(spans):
            own = slice(c * SPAN, (c + 1) * SPAN)
            span_keys = slice(c * keys, (c + 1) * keys)
            parts = []
            for p in range(pairs):
                cut = slice(2 * HEAD_DIM * p, 2 * HEAD_DIM * (p + 1))
                weights, total = softmax(dot_nt(stacked(cq[own, cut]), ck[span_keys, cut]))
                lse[2, own, 2 * p : 2 * p + 1] = total[:SPAN]
                lse[2, own, 2 * p + 1 : 2 * p + 2] = total[SPAN:]
                parts.append(merged(dot(weights.astype(BF), cv[span_keys, cut])))
            outs.append(jnp.concatenate(parts, axis=1))
        os_[1] = shift_down(jnp.concatenate(outs, axis=0)).astype(BF)
        arrived((1, "out"))
        k = exchange_start(lambda c: dot(os_[1], wo[1, :, pieces[c]]))
        send_attended(1)
        return k

    def cross_backward():
        low = hbuf[...].astype(BF)
        send_upstream(1, low)
        dos[...] = shift_up(dot_nt(low, wo[1])).astype(BF)
        query_grads = []
        for c in range(spans):
            own = slice(c * SPAN, (c + 1) * SPAN)
            span_keys = slice(c * keys, (c + 1) * keys)
            parts = []
            for p in range(pairs):
                cut = slice(2 * HEAD_DIM * p, 2 * HEAD_DIM * (p + 1))
                q2 = stacked(cq[own, cut])
                do2 = stacked(dos[own, cut])
                scores = dot_nt(q2, ck[span_keys, cut])
                total = jnp.concatenate(
                    [lse[2, own, 2 * p : 2 * p + 1], lse[2, own, 2 * p + 1 : 2 * p + 2]], axis=0
                )
                weights = jnp.exp(scores - total)
                grads = dot_nt(do2, cv[span_keys, cut])
                inner = jnp.sum(weights * grads, axis=-1, keepdims=True)
                score_grad = (weights * (grads - inner)).astype(BF)
                parts.append(SCALE * merged(dot(score_grad, ck[span_keys, cut])))
                dkn[span_keys, cut] = dot_tn(score_grad, q2).astype(BF)
                dvn[span_keys, cut] = dot_tn(weights.astype(BF), do2).astype(BF)
            query_grads.append(jnp.concatenate(parts, axis=1))
        dqk[1, :, :width] = shift_down(jnp.concatenate(query_grads, axis=0)).astype(BF)
        send_grads(1)
        k = exchange_start(whole(dot_nt(dqk[1, :, :width], unit(1, 0, 0, width))))

        sm[12:13, :] = column_sum(low)
        sm[20:21, :width] = column_sum(dqk[1, :, :width])
        sm[21:22, :width] = column_sum(dvn[...])
        return k

    def neighbours_start():
        def feature_half(which):
            key_rows = units[1, 0, which, :, :, :, :, second].reshape(dim // 2, width)
            value_rows = units[1, 1, which, :, :, :, :, first].reshape(dim // 2, width)
            return dot_nt(dkn[...], key_rows) + dot_nt(dvn[...], value_rows)

        given = feature_half(1 - t).astype(BF)
        for q in range(ff // width):
            gp[1, :, q * width : (q + 1) * width] = given[q * rows : (q + 1) * rows]
        other = push(gp.at[1], gp.at[0], sib)
        nbr_sum[0] = (other, feature_half(t).astype(BF))

    def send_half(which, columns, name):
        a = axis_of(1, which)
        at = (1, which) + half_at(a, 1 - bits[a]) + (slice(None),) * a + (slice(None), columns)
        factors[name] = push(units.at[at], rx0.at[which], partner[a])

    def cross_key_weights():
        unit_store(1, 0, width, dot_tn(nsel[...], dkn[...]))
        send_half(0, second, "k")

    def cross_value_weights():
        unit_store(1, 1, 0, dot_tn(nsel[...], dvn[...]))
        send_half(1, first, "v")

    nbr_sum = [None]

    def neighbours_end():
        other, keep = nbr_sum[0]
        other.wait_recv()
        first_store = len(stores)
        taken = [gp[0, :, q * width : (q + 1) * width].astype(F32) for q in range(ff // width)]
        total = keep.astype(F32) + jnp.concatenate(taken, axis=0)
        for slot in range(pool):
            summed = jnp.zeros((length, total.shape[1]), F32)
            for pick in range(pool):
                hit = jnp.where(assign[pick % 2, pick // 2] == slot, F32(1.0), F32(0.0))
                summed += hit * total[pick * length : (pick + 1) * length]
            place = slot % nbr_o.shape[0]
            if slot >= nbr_o.shape[0]:
                stores[first_store + place].wait()
                stores[first_store + place] = None
            nbr_o[place] = summed
            store(nbr_o.at[place], nbr_h.at[slot])

    cuts = [slice(c * dim, (c + 1) * dim) for c in range(ff // dim)]

    def mlp_forward(j):
        if j == 0:
            arrived("mlp0")
        part = None
        for cut in cuts[:-1]:
            pre = dot(ag[2 * j, 0], win[j, :, cut]) + in_b[j : j + 1, cut]
            active, slope = gelu_parts(pre)
            gp[j, :, cut] = slope.astype(BF)
            term = dot(active.astype(BF), wout[j, cut, :])
            part = term if part is None else part + term
        cut = cuts[-1]
        pre = dot(ag[2 * j, 0], win[j, :, cut]) + in_b[j : j + 1, cut]
        active, slope = gelu_parts(pre)
        gp[j, :, cut] = slope.astype(BF)
        active = active.astype(BF)
        return exchange_start(lambda c: whole(part)(c) + dot(active, wout[j, cut, pieces[c]]))

    def down_early():
        for q in range(ff // width):
            cut = slice(q * width, (q + 1) * width)
            dkn[q * rows : (q + 1) * rows, :] = dot_nt(ag[3, 0], wout[1, cut, :]).astype(BF)

    def mlp_backward(j, before=None):
        low = ag[2 * j + 1, 0]
        sm[13 + j : 14 + j, :] = column_sum(low)
        grads = []
        for c, cut in enumerate(cuts):
            if j == 1:
                per = dim // width
                down = jnp.concatenate(
                    [
                        dkn[q * rows : (q + 1) * rows, :].astype(F32)
                        for q in range(c * per, (c + 1) * per)
                    ],
                    axis=1,
                )
            else:
                down = dot_nt(low, wout[j, cut, :])
            pre_grad = (down * gp[j, :, cut].astype(F32)).astype(BF)
            grads.append(pre_grad)
        part = None
        for pre_grad, cut in zip(grads[:-1], cuts[:-1]):
            term = dot_nt(pre_grad, win[j, :, cut])
            part = term if part is None else part + term
        if before is not None:
            before()
        k = exchange_start(
            lambda c: whole(part)(c) + dot_nt(grads[-1], win[j, pieces[c], cuts[-1]])
        )
        for c, pre_grad in enumerate(grads):
            sm[24 + 2 * j + c : 25 + 2 * j + c, :] = column_sum(pre_grad)
        return k

    def mlp_rows(j):
        gather_wait(2 * j)
        gather_wait(2 * j + 1)

        def bucket(b, carry):
            for c in range(2):
                turn(turned, ag[2 * j + c, b])
                part = turned[:, :, y, x] if j == 0 else turned[z1, z0]
                turned_rows[c, b] = part.reshape(4 * block, rows)
            return carry

        lax.fori_loop(0, 4, bucket, 0)

    def mlp_weights(j, c):
        cut = cuts[c]
        acc[...] = jnp.zeros_like(acc)

        def bucket(b, carry):
            pre = dot(ag[2 * j, b], win[j, :, cut]) + in_b[j : j + 1, cut]
            active, slope = gelu_parts(pre)
            pre_grad = (dot_nt(ag[2 * j + 1, b], wout[j, cut, :]) * slope).astype(BF)
            acc[0] += dot(turned_rows[0, b], pre_grad)
            acc[1] += dot(turned_rows[1, b], active.astype(BF))
            return carry

        lax.fori_loop(0, 4, bucket, 0)
        zst[j, c] = acc[...].astype(BF).reshape(2, 2, 2, block, dim)
        if j == 0:
            chain = Chain(lambda s: zst.at[0, c, :, s // 2, s % 2], rz.at[c])
            scatter["z", c] = chain
            chain.first()
        elif c == 0:
            scatter["w", c] = push(zst.at[1, c, :, :, 1 - x], rw0.at[c], px)
        else:
            scatter["w", c] = push(zst.at[1, c, :, 1 - y], rw0.at[c], py)

    def mlp_second(c):
        scatter["w", c].wait_recv()
        got = rw0[c].astype(F32)
        if c == 0:
            zst[1, c, :, :, x] = (zst[1, c, :, :, x].astype(F32) + got).astype(BF)
            scatter["w", c] = push(zst.at[1, c, :, 1 - y, x], rw1.at[c], py)
        else:
            zst[1, c, :, y] = (zst[1, c, :, y].astype(F32) + got).astype(BF)
            scatter["w", c] = push(zst.at[1, c, :, y, 1 - x], rw1.at[c], px)

    def mlp_end(j, c):
        if j == 0:
            scatter["z", c].end(gm_o.at[j, c])
        else:
            scatter["w", c].wait_recv()
            gm_o[j, c] = zst[1, c, :, y, x].astype(F32) + rw1[c].astype(F32)
        store(gm_o.at[j, c], gm_h.at[j, :, :, pl.ds(c * dim, dim)])

    live = lax.broadcasted_iota(jnp.int32, (rows, dim), 0) < lengths[0]
    sm[...] = jnp.zeros_like(sm)
    hbuf[...] = hidden[...].astype(F32)
    norm_forward(0, into_us(0))
    k = self_forward(0)
    send_inputs(0)
    arrived("cot")
    ag[3, 0] = jnp.where(live, ag[3, 0], jnp.zeros((rows, dim), BF))
    gather_start(3, (pz0, pz1, pz))
    cross_keys()
    hbuf[...] += exchange_wait(k) + sa_ob[0:1, :]
    norm_forward(1, into_us(1))
    k = cross_forward()
    send_inputs(1)
    hbuf[...] += exchange_wait(k) + ca_ob[...].reshape(1, dim)
    norm_forward(2, into_ag(0))
    gather_start(0)
    k = mlp_forward(0)
    arrived("mlp1")
    down_early()
    hbuf[...] += exchange_wait(k) + out_b[0:1, :]
    norm_forward(3, into_us(2))
    k = self_forward(1)
    send_inputs(2)
    hbuf[...] += exchange_wait(k) + sa_ob[1:2, :]
    norm_forward(4, into_ag(2))
    gather_start(2, (pz0, pz1, pz))
    last = mlp_forward(1)
    gather_forward(0)

    small_copy = []
    small_bufs = [sm] + [small_o.at[q] for q in range(4)]

    def small_step(k):
        if k:
            small_copy[-1].wait_recv()
            small_bufs[k][...] = small_bufs[k - 1][...] + rsm[k - 1]
        if k < 4:
            small_copy.append(push(small_bufs[k], rsm.at[k], (px, py, pz0, pz1)[k]))
            return
        small = small_o.at[3]
        gain_o[...] = small[0:5, :]
        bias_o[...] = small[5:10, :]
        sa_ob_o[...] = small[10:12, :]
        ca_ob_o[...] = small[12, :]
        out_b_o[...] = small[13:15, :]
        for j in range(2):
            sa_b_o[j] = small[16 + 2 * j : 18 + 2 * j, :width]
            for c, cut in enumerate(cuts):
                in_b_o[j : j + 1, cut] = small[24 + 2 * j + c : 25 + 2 * j + c, :]
        ca_b_o[...] = small[20:22, :width]
        for src, dst in (
            (gain_o, gain_h), (bias_o, bias_h), (sa_ob_o, sa_ob_h), (ca_ob_o, ca_ob_h),
            (out_b_o, out_b_h), (sa_b_o, sa_b_h), (ca_b_o, ca_b_h), (in_b_o, in_b_h),
        ):
            store(src, dst)

    pending = {}

    def begin(norm, call, *args):
        pending[norm] = call(*args)

    def finish_norm(norm):
        norm_backward(norm, exchange_wait(pending[norm]))

    def first_grads():
        ag[1, 0] = hbuf[...].astype(BF)
        gather_start(1, (px, py, pxy))

    def last_norm():
        finish_norm(0)
        store(hbuf, grad_h)

    def feed_forward_back():
        def output():
            final = hbuf[...] + exchange_wait(last) + out_b[1:2, :]
            hid_o[...] = jnp.where(live, final, 0.0).astype(BF)
            store(hid_o, hid_h)
            hbuf[...] = ag[3, 0].astype(F32)

        begin(4, mlp_backward, 1, output)
        finish_norm(4)

    steps = {
        "b1": feed_forward_back,
        "b0a": partial(begin, 2, mlp_backward, 0),
        "b0b": partial(finish_norm, 2),
        "S2a": partial(begin, 3, self_backward, 1),
        "S2b": partial(finish_norm, 3),
        "S0a": partial(begin, 0, self_backward, 0),
        "S0b": last_norm,
        "d1": first_grads,
        "g2": lambda: send_grads(2),
        "Ca": partial(begin, 1, cross_backward),
        "Cb": partial(finish_norm, 1),
        "Cn": neighbours_start,
        "Ck": cross_key_weights,
        "Cv": cross_value_weights,
        "gswd2": lambda: gather_swap(3),
        "gswd1": lambda: gather_swap(1),
        "gswu2": lambda: gather_swap(2),
        "gru1": lambda: gather_relay(0),
        "rows0": lambda: mlp_rows(0),
        "rows1": lambda: mlp_rows(1),
        "nbr": neighbours_end,
    }
    for n in range(5):
        steps["sm%d" % n] = partial(small_step, n)
    for n in range(2):
        steps["mw0%d" % n] = partial(mlp_weights, 0, n)
        steps["mw1%d" % n] = partial(mlp_weights, 1, n)
        steps["mz2%d" % n] = lambda n=n: scatter["z", n].second()
        steps["mz3%d" % n] = lambda n=n: scatter["z", n].third()
        steps["mze%d" % n] = partial(mlp_end, 0, n)
        steps["ms%d" % n] = partial(mlp_second, n)
        steps["me%d" % n] = partial(mlp_end, 1, n)
    for layer in range(3):
        steps["rf%d" % layer] = partial(relay_factors, layer)
        for n in range(2):
            steps["s1%s%d" % ("ab"[n], layer)] = partial(scatter_one, layer, n)
            steps["s2%d%d" % (layer, n)] = partial(scatter_two, layer, n)
            steps["s3%d%d" % (layer, n)] = partial(scatter_three, layer, n)
            steps["s4%d%d" % (layer, n)] = partial(scatter_four, layer, n)
            steps["se%d%d" % (layer, n)] = partial(scatter_end, layer, n)
    for name in ORDER:
        steps[name]()
    for copy in stores:
        if copy is not None:
            copy.wait()
    for copy in sends:
        copy.wait_send()
    for chain in chains:
        chain.sent()
    for k in (ex[0] - 2, ex[0] - 1):
        for copy in ex_copy[k]:
            copy.wait_send()


def finish(*refs):
    parts, outs = refs[:13], refs[13:30]
    held, get, put = refs[30:43], refs[43], refs[44]
    (
        hid_o, grad_o, nbr_o, gain_o, bias_o, sa_qkv_o, sa_b_o, sa_out_o, sa_ob_o, ca_qkv_o,
        ca_b_o, ca_out_o, ca_ob_o, in_o, in_b_o, out_o, out_b_o,
    ) = outs
    width = ca_out_o.shape[1]
    ga, gm = held[3], held[4]
    places = {
        0: [(held[0], hid_o)],
        1: [(held[1], grad_o)],
        2: [(held[2], nbr_o)],
        3: [],
        4: [(gm.at[j, c], out.at[j]) for j in range(2) for c, out in enumerate((in_o, out_o))],
    }
    for a, out, rows in (
        (0, sa_qkv_o.at[0], sa_out_o.at[0]), (1, ca_qkv_o, ca_out_o),
        (2, sa_qkv_o.at[1], sa_out_o.at[1]),
    ):
        for c in range(4):
            src = ga.at[a, c // 2, :, pl.ds(c % 2 * width, width)]
            places[3].append((src, rows if c == 3 else out.at[c]))
    for k, out in enumerate((gain_o, bias_o, sa_ob_o, ca_ob_o, out_b_o, sa_b_o, ca_b_o, in_b_o)):
        places[5 + k] = [(held[5 + k], out)]
    order = (2, 4, 3, 1, 0) + tuple(range(5, 13))
    fetched = {}
    for k in order:
        fetched[k] = pltpu.make_async_copy(parts[k], held[k], get.at[k])
        fetched[k].start()
    copies = []
    for k in order:
        fetched[k].wait()
        for src, dst in places[k]:
            copies.append(pltpu.make_async_copy(src, dst, put.at[len(copies)]))
            copies[-1].start()
    for copy in copies:
        copy.wait()


def on_device(
    n_dp,
    hidden_in, lengths, neighbours, assign, cotangent, norm_gain, norm_bias, sa_qkv, sa_bias,
    sa_out, sa_out_bias, ca_qkv, ca_bias, ca_out, ca_out_bias, mlp_in, mlp_in_bias, mlp_out,
    mlp_out_bias,
):
    rows, dim = hidden_in.shape
    width = sa_out.shape[1]
    ff = mlp_in.shape[2]
    pool, length = neighbours.shape[0], neighbours.shape[1]
    block = dim // GROUPS
    picks = assign.size * length
    vmem = pl.BlockSpec(memory_space=pltpu.VMEM)
    smem = pl.BlockSpec(memory_space=pltpu.SMEM)
    hbm = pl.BlockSpec(memory_space=pl.ANY)

    def array(*shape, dtype=F32):
        return jax.ShapeDtypeStruct(shape, dtype)

    outs = (
        array(rows, dim, dtype=BF),
        array(rows, dim),
        array(pool, length, width),
        array(3, 2, block, 2 * width),
        array(2, 2, block, ff),
        array(5, dim),
        array(5, dim),
        array(2, dim),
        array(dim),
        array(2, dim),
        array(2, 2, width),
        array(2, width),
        array(2, ff),
    )
    V = pltpu.VMEM
    scratch = [
        V((rows, dim), BF),
        V((pool // 2, length, width), F32),
        V((3, 2, block, 2 * width), F32),
        V((2, ff // dim, 2, block, dim), F32),
        V((4, SMALL_ROWS, dim), F32),
    ] + [V(out.shape, F32) for out in outs[5:]] + [
        V((3, 2, 2, 2, 2, 2, block, 2 * width), BF),
        V((3, width, dim), BF),
        V((2, dim, ff), BF),
        V((2, ff, dim), BF),
        V((picks, dim), BF),
        V((4, 4, rows, dim), BF),
        V((3, rows, dim), BF),
        V((5, rows, dim), BF),
        V((rows, 128), F32),
        V((2, rows, width), BF),
        V((2, rows, width), BF),
        V((2, rows, width), BF),
        V((3, rows, width), BF),
        V((rows, width), BF),
        V((picks, width), BF),
        V((picks, width), BF),
        V((3, rows, 128), F32),
        V((2, rows, ff), BF),
        V((3, rows, 2 * width), BF),
        V((2, rows, width), BF),
        V((picks, width), BF),
        V((picks, width), BF),
        V((rows, width), BF),
        V((2, rows, dim), BF),
        V((2, rows, dim), BF),
        V((2, 2, 2, 2, block, width), BF),
        V((3, 2, 2, 2, block, 2 * width), BF),
        V((3, 2, 5, block, 2 * width), BF),
        V((2, 4 * block, dim), F32),
        V((2, ff // dim, 2, 2, 2, block, dim), BF),
        V((ff // dim, 5, 2, block, dim), BF),
        V((ff // dim, 2, 2, block, dim), BF),
        V((ff // dim, 2, block, dim), BF),
        V((SMALL_ROWS, dim), F32),
        V((4, SMALL_ROWS, dim), F32),
        V((rows, dim), F32),
        V((3, 2, 2, 2, 2, block, rows), BF),
        V((3, 2, 2, 2, 2, block, rows), BF),
        V((3, 2, 2, 2, block, rows), BF),
        V((2, 2, 2, 2, block, rows), BF),
        V((3, 2, 2, 2, block, rows), BF),
        V((3, rows, width), BF),
        V((3, rows, 2 * width), BF),
        V((2, rows, width), BF),
        V((2, 2, 2, 2, block, rows), BF),
        V((2, 4, 4 * block, rows), BF),
        pltpu.SemaphoreType.DMA((64,)),
        pltpu.SemaphoreType.DMA((160,)),
        pltpu.SemaphoreType.DMA((160,)),
    ]
    hid, grad, nbr, ga, gm, *small = pl.pallas_call(
        partial(kernel, n_dp),
        out_shape=outs,
        in_specs=[smem] * 2 + [vmem] * 9 + [hbm] * 8,
        out_specs=(hbm,) * 13,
        scratch_shapes=scratch,
        compiler_params=pltpu.CompilerParams(
            collective_id=0, has_side_effects=True, vmem_limit_bytes=64 * 1024 * 1024 - 65536
        ),
    )(
        lengths, assign.T, norm_gain, norm_bias, sa_bias, sa_out_bias,
        ca_bias, ca_out_bias, mlp_in_bias, mlp_out_bias,
        hidden_in, cotangent, neighbours, sa_qkv, sa_out, ca_qkv, ca_out, mlp_in, mlp_out,
    )
    rest = n_dp // GROUPS
    if rest > 1:
        members = [[a * rest + b for b in range(rest)] for a in range(GROUPS)]
        ga = lax.psum_scatter(ga, "dp", scatter_dimension=2, axis_index_groups=members, tiled=True)
        gm = lax.psum_scatter(gm, "dp", scatter_dimension=2, axis_index_groups=members, tiled=True)
        small = lax.psum(small, "dp", axis_index_groups=members)
    owned = block // rest
    results = pl.pallas_call(
        finish,
        out_shape=(
            outs[0],
            outs[1],
            outs[2],
            array(5, dim),
            array(5, dim),
            array(2, 3, owned, width),
            array(2, 2, width),
            array(2, owned, width),
            array(2, dim),
            array(3, owned, width),
            array(2, width),
            array(owned, width),
            array(dim),
            array(2, owned, ff),
            array(2, ff),
            array(2, owned, ff),
            array(2, dim),
        ),
        in_specs=[hbm] * 13,
        out_specs=(hbm,) * 17,
        scratch_shapes=[
            V((rows, dim), BF),
            V((rows, dim), F32),
            V((pool, length, width), F32),
            V((3, 2, owned, 2 * width), F32),
            V((2, 2, owned, ff), F32),
        ]
        + [V(out.shape, F32) for out in outs[5:]]
        + [pltpu.SemaphoreType.DMA((16,)), pltpu.SemaphoreType.DMA((32,))],
    )(hid, grad, nbr, ga, gm, *small)
    results = list(results)
    for k in (7, 11, 15):
        results[k] = results[k].swapaxes(-1, -2)
    return tuple(results)


def solution(mesh):
    return jax.shard_map(
        partial(on_device, mesh.shape["dp"]),
        mesh=mesh,
        in_specs=(
            P("dp", None),
            P("dp"),
            P("dp", None, None),
            P("dp", None),
            P("dp", None),
            P(),
            P(),
            P(None, None, None, "tensor"),
            P(None, None, "tensor"),
            P(None, "tensor", None),
            P(),
            P(None, None, "tensor"),
            P(None, "tensor"),
            P("tensor", None),
            P(),
            P(None, None, "tensor"),
            P(None, "tensor"),
            P(None, "tensor", None),
            P(),
        ),
        out_specs=(
            P("dp", None),
            P("dp", None),
            P("dp", None, "tensor"),
            P(),
            P(),
            P(None, None, "dp", "tensor"),
            P(None, None, "tensor"),
            P(None, "tensor", "dp"),
            P(),
            P(None, "dp", "tensor"),
            P(None, "tensor"),
            P("tensor", "dp"),
            P(),
            P(None, "dp", "tensor"),
            P(None, "tensor"),
            P(None, "tensor", "dp"),
            P(),
        ),
        check_vma=False,
    )
```

```python
from functools import partial

import jax
import jax.numpy as jnp
from jax import lax
from jax.experimental import pallas as pl
from jax.experimental.pallas import tpu as pltpu
from jax.sharding import PartitionSpec as P

HEAD_DIM = 64
SPAN = 64
GROUPS = 16
EPSILON = 1e-05
SCALE = 0.125
MASKED = -1e30
MESH = pl.DeviceIdType.MESH
BF = jnp.bfloat16
F32 = jnp.float32
SMALL_ROWS = 32
ORDER = (
    "b1", "S2a", "S2b", "d1", "b0a", "gswd2", "b0b", "g2", "Ca", "gru1", "Cn", "gswd1", "Cv", "Ck",
    "rows0", "rf2", "mw01", "rf1", "s1a2", "mw00", "Cb", "S0a", "mz21", "gswu2", "rf0", "S0b",
    "s1b2", "s1b0", "s1a1", "s220", "sm0", "s1a0", "mz20", "rows1", "s1b1", "s221", "s320", "mw11",
    "s201", "s321", "mz31", "s420", "mz30", "mw10", "s210", "s200", "s301", "nbr", "s310", "s211",
    "s421", "sm1", "s300", "ms1", "s410", "s401", "ms0", "mze0", "sm2", "s311", "s400", "sm3",
    "se01", "mze1", "se21", "s411", "me1", "se10", "se00", "se20", "sm4", "me0", "se11",
)


def dot(a, b):
    return jnp.dot(a, b, preferred_element_type=F32)


def dot_nt(a, b):
    return lax.dot_general(a, b, (((1,), (1,)), ((), ())), preferred_element_type=F32)


def dot_tn(a, b):
    return lax.dot_general(a, b, (((0,), (0,)), ((), ())), preferred_element_type=F32)


def column_sum(values):
    return jnp.sum(values.astype(F32), axis=0, keepdims=True)


def gelu_parts(a):
    phi = 0.5 * (1.0 + lax.erf(a * 0.7071067811865476))
    density = 0.3989422804014327 * jnp.exp(-0.5 * a * a)
    return a * phi, phi + a * density


def kernel(n_dp, *refs):
    (
        lengths, assign, gain, bias, sa_b, sa_ob, ca_b, ca_ob, in_b, out_b,
        hidden, cot, n_ref, w_sa_qkv, w_sa_out, w_ca_qkv, w_ca_out, w_in, w_out,
        hid_h, grad_h, nbr_h, ga_h, gm_h, gain_h, bias_h, sa_ob_h, ca_ob_h, out_b_h, sa_b_h, ca_b_h,
        in_b_h,
        hid_o, nbr_o, ga_o, gm_o, small_o, gain_o, bias_o, sa_ob_o, ca_ob_o, out_b_o, sa_b_o, ca_b_o,
        in_b_o,
        units, wo, win, wout, nsel, ag, us, xh, rstd, qs, ks, vs, os_, cq, ck, cv,
        lse, gp, dqk, dvs, dkn, dvn, dos, xs, xr, rx0, rx1, rx2,
        acc, zst, rz, rw0, rw1, sm, rsm, hbuf,
        ut, dt, rut_x, rut_y, rdt, ro, rdqk, rdv, turned, turned_rows,
        lsem, ssem, rsem,
    ) = refs
    rows, dim = hbuf.shape
    width = wo.shape[1]
    ff = win.shape[2]
    block = dim // GROUPS
    half = rows // 2
    i = lax.axis_index("dp")
    t = lax.axis_index("tensor")
    m = n_dp // GROUPS
    g = i // m
    r = i % m
    x = g % 2
    y = (g // 2) % 2
    z0 = (g // 4) % 2
    z1 = g // 8
    px = ((g + 1 - 2 * x) * m + r, t)
    py = ((g + 2 - 4 * y) * m + r, t)
    pxy = ((g + 3 - 2 * x - 4 * y) * m + r, t)
    pz0 = ((g + 4 - 8 * z0) * m + r, t)
    pz1 = ((g + 8 - 16 * z1) * m + r, t)
    pz = ((g + 12 - 8 * z0 - 16 * z1) * m + r, t)
    zz = g // 4
    sib = (i, 1 - t)
    count = [0, 0]
    sends = []

    def load(src, dst):
        copy = pltpu.make_async_copy(src, dst, lsem.at[count[0]])
        count[0] += 1
        copy.start()
        return copy

    stores = []

    def store(src, dst):
        stores.append(load(src, dst))

    def push(src, dst, to):
        k = count[1]
        count[1] += 1
        copy = pltpu.make_async_remote_copy(
            src_ref=src, dst_ref=dst, send_sem=ssem.at[k], recv_sem=rsem.at[k],
            device_id=to, device_id_type=MESH,
        )
        copy.start()
        sends.append(copy)
        return copy

    loads = {}

    def load_attention(layer, src):
        def blocks(c):
            return src(c).reshape(2, 2, 2, 2, block, width)

        loads[layer, "qkv"] = [
            load(blocks(0), units.at[layer, 0, :, :, :, :, :, pl.ds(0, width)]),
            load(blocks(1), units.at[layer, 0, :, :, :, :, :, pl.ds(width, width)]),
            load(blocks(2), units.at[layer, 1, :, :, :, :, :, pl.ds(0, width)]),
        ]

    load_attention(0, lambda c: w_sa_qkv.at[0, c])
    loads[0, "out"] = [load(w_sa_out.at[0], wo.at[0])]
    loads["cot"] = [load(cot, ag.at[3, 0])]
    load_attention(1, lambda c: w_ca_qkv.at[c])
    pool, length = n_ref.shape[0], n_ref.shape[1]
    loads["n"] = [
        load(n_ref.at[:, :, pl.ds(c * width, width)], into.reshape(pool, length, width))
        for c, into in enumerate((dkn, dvn))
    ]
    loads[1, "out"] = [load(w_ca_out, wo.at[1])]
    loads["mlp0"] = [load(w_in.at[0], win.at[0]), load(w_out.at[0], wout.at[0])]
    load_attention(2, lambda c: w_sa_qkv.at[1, c])
    loads[2, "out"] = [load(w_sa_out.at[1], wo.at[2])]
    loads["mlp1"] = [load(w_in.at[1], win.at[1]), load(w_out.at[1], wout.at[1])]

    def arrived(key):
        for copy in loads[key]:
            copy.wait()

    barrier = pltpu.get_barrier_semaphore()
    partners = (sib, px, py, pxy, pz0, pz1, pz)
    for to in partners:
        pl.semaphore_signal(barrier, inc=1, device_id=to, device_id_type=MESH)

    def entered():
        pl.semaphore_wait(barrier, len(partners))

    def unit(layer, which, first, size):
        value = units[layer, which, :, :, :, :, :, pl.ds(first, size)]
        return value.reshape(dim, size)

    def unit_store(layer, which, first, value):
        size = value.shape[1]
        units[layer, which, :, :, :, :, :, pl.ds(first, size)] = value.astype(BF).reshape(
            2, 2, 2, 2, block, size
        )

    ex = [0]
    ex_copy = {}

    pieces = (pl.ds(0, 2 * dim // 3), pl.ds(2 * dim // 3, dim // 3))

    def exchange_start(part):
        k = ex[0]
        ex[0] += 1
        slot = k % 2
        ex_copy[k] = []
        for c, columns in enumerate(pieces):
            if k >= 2:
                ex_copy[k - 2][c].wait_send()
            xs[slot, :, columns] = part(c).astype(BF)
            copy = pltpu.make_async_remote_copy(
                src_ref=xs.at[slot, :, columns], dst_ref=xr.at[slot, :, columns],
                send_sem=ssem.at[156 + 2 * slot + c], recv_sem=rsem.at[156 + 2 * slot + c],
                device_id=sib, device_id_type=MESH,
            )
            copy.start()
            ex_copy[k].append(copy)
        return k

    def whole(part):
        return lambda c: part[:, pieces[c].start : pieces[c].start + pieces[c].size]

    def exchange_wait(k):
        for copy in ex_copy[k]:
            copy.wait_recv()
        return xs[k % 2].astype(F32) + xr[k % 2].astype(F32)

    gathers = {}

    mine = pl.ds(pl.multiple_of(t * half, half), half)
    quarter = half // 2
    upper = pl.ds(pl.multiple_of(t * half, quarter), quarter)
    lower = pl.ds(pl.multiple_of(t * half + quarter, quarter), quarter)

    def gather_start(a, peers=(px, py)):
        gathers[a] = [
            push(ag.at[a, 0, mine], ag.at[a, p + 1, mine], to) for p, to in enumerate(peers)
        ]

    def gather_swap(a):
        for copy in gathers[a]:
            copy.wait_recv()
        gathers[a] = [push(ag.at[a, p, mine], ag.at[a, p, mine], sib) for p in (1, 2, 3)]

    def gather_forward(a):
        for copy in gathers[a]:
            copy.wait_recv()
        gathers[a] = [
            push(ag.at[a, 1, upper], ag.at[a, 3, upper], py),
            push(ag.at[a, 2, lower], ag.at[a, 3, lower], px),
        ] + [push(ag.at[a, p, mine], ag.at[a, p, mine], sib) for p in (1, 2)]

    def gather_relay(a):
        for copy in gathers[a][:2]:
            copy.wait_recv()
        gathers[a] = gathers[a][2:] + [push(ag.at[a, 3, mine], ag.at[a, 3, mine], sib)]

    def gather_wait(a):
        for copy in gathers[a]:
            copy.wait_recv()

    UP, DOWN = {1: 0, 2: 1, 3: 2}, {0: 3, 1: 4, 2: 0}
    above = ((g + 4) * m + r, t)
    below = ((g - 4) * m + r, t)
    chains = []

    class Chain:
        def __init__(self, shard, into):
            self.base = count[1]
            count[1] += 5
            self.shard, self.into = shard, into
            chains.append(self)

        def copy(self, s, slot, to):
            return pltpu.make_async_remote_copy(
                src_ref=self.shard(s), dst_ref=self.into.at[slot],
                send_sem=ssem.at[self.base + slot], recv_sem=rsem.at[self.base + slot],
                device_id=to, device_id_type=MESH,
            )

        def arrive(self, s, slot):
            self.copy(s, slot, above).wait_recv()
            return self.into[slot].astype(F32)

        def pass_on(self, s, slot, to):
            own = self.shard(s)
            own[...] = (own[...].astype(F32) + self.arrive(s, slot)).astype(BF)
            self.copy(s, slot, to).start()

        def first(self):
            @pl.when(zz == 0)
            def _():
                for s in (3, 2, 1):
                    self.copy(s, UP[s], above).start()

            @pl.when(zz == 3)
            def _():
                for s in (0, 1, 2):
                    self.copy(s, DOWN[s], below).start()

        def second(self):
            @pl.when(zz == 1)
            def _():
                for s in (3, 2):
                    self.pass_on(s, UP[s], above)

            @pl.when(zz == 2)
            def _():
                for s in (0, 1):
                    self.pass_on(s, DOWN[s], below)

        def third(self):
            @pl.when(zz == 2)
            def _():
                self.pass_on(3, UP[3], above)

            @pl.when(zz == 1)
            def _():
                self.pass_on(0, DOWN[0], below)

        def end(self, out):
            for s in range(4):
                @pl.when(zz == s)
                def _(s=s):
                    total = self.shard(s)[...].astype(F32)
                    if s > 0:
                        total += self.arrive(s, UP[s])
                    if s < 3:
                        total += self.arrive(s, DOWN[s])
                    out[...] = total

        def sent(self):
            for z, slots in enumerate(
                ((UP[1], UP[2], UP[3]), (UP[2], UP[3], DOWN[0]),
                 (UP[3], DOWN[0], DOWN[1]), (DOWN[0], DOWN[1], DOWN[2]))
            ):
                @pl.when(zz == z)
                def _(slots=slots):
                    for slot in slots:
                        self.copy(0, slot, above).wait_send()

    def turn(dst, value):
        dst[...] = value.T.reshape(2, 2, 2, 2, block, rows)

    scatter = {}
    factors = {}

    bits, partner = (x, y), (px, py)

    def axis_of(layer, which):
        return 1 - which if layer == 0 else which

    def half_at(a, v):
        return (slice(None),) * (3 - a) + (v,)

    def quarter_at(a, v, w):
        return (slice(None), slice(None)) + ((w, v) if a == 0 else (v, w))

    def send_inputs(layer):
        turn(ut.at[layer], us[layer])
        for name, which, into in (("u0", 0, rut_x), ("u1", 1, rut_y)):
            if name == "u1" and layer == 1:
                continue
            a = axis_of(layer, which)
            place = layer if which == 0 else layer // 2
            factors[layer, name] = push(
                ut.at[(layer, t) + half_at(a, 1 - bits[a])[1:]], into.at[place, t], partner[a]
            )

    def send_attended(layer):
        factors[layer, "o"] = push(os_.at[layer], ro.at[layer], partner[axis_of(layer, 1)])

    def send_upstream(layer, low):
        turn(dt.at[layer], low)
        a = axis_of(layer, 1)
        factors[layer, "d"] = push(
            dt.at[(layer, t) + half_at(a, 1 - bits[a])[1:]], rdt.at[layer, t], partner[a]
        )

    def relay_factor(layer, name):
        into = {"u0": rut_x.at[layer, t], "u1": rut_y.at[layer // 2, t], "d": rdt.at[layer, t]}
        factors[layer, name].wait_recv()
        factors[layer, name] = push(into[name], into[name], sib)

    def relay_factors(layer):
        relay_factor(layer, "u0")
        if layer != 1:
            relay_factor(layer, "u1")
        relay_factor(layer, "d")

    def send_grads(layer):
        to = partner[axis_of(layer, 0)]
        if layer == 1:
            factors[layer, "0"] = push(
                dqk.at[layer, :, pl.ds(0, width)], rdqk.at[layer, :, pl.ds(0, width)], to
            )
        else:
            factors[layer, "0"] = push(dqk.at[layer], rdqk.at[layer], to)
            factors[layer, "1"] = push(
                dvs.at[layer // 2], rdv.at[layer // 2], partner[axis_of(layer, 1)]
            )

    first, second = pl.ds(0, width), pl.ds(width, width)

    def scatter_one(layer, which):
        a = axis_of(layer, which)
        mine_at = half_at(a, bits[a])
        unit_at = (layer, which) + mine_at + (slice(None),) * a

        def put(columns, total):
            units[unit_at + (slice(None), columns)] = total.astype(BF).reshape(
                2, 2, 2, block, total.shape[1]
            )

        def rows_of(ref):
            return ref[(layer,) + mine_at].reshape(dim // 2, rows)

        def add(name, columns):
            factors[name].wait_recv()
            at = unit_at + (slice(None), columns)
            units[at] = (units[at].astype(F32) + rx0[which].astype(F32)).astype(BF)

        if which == 0:
            for name in ("u0", "0"):
                factors[layer, name].wait_recv()
            size = width if layer == 1 else 2 * width
            put(
                pl.ds(0, size),
                dot(rows_of(ut), dqk[layer, :, :size])
                + dot(rut_x[layer].reshape(dim // 2, rows), rdqk[layer, :, :size]),
            )
            if layer == 1:
                add("k", second)
        else:
            if layer == 1:
                add("v", first)
            else:
                for name in ("u1", "1"):
                    factors[layer, name].wait_recv()
                put(
                    first,
                    dot(rows_of(ut), dvs[layer // 2])
                    + dot(rut_y[layer // 2].reshape(dim // 2, rows), rdv[layer // 2]),
                )
            for name in ("o", "d"):
                factors[layer, name].wait_recv()
            put(
                second,
                dot(rows_of(dt), os_[layer])
                + dot(rdt[layer].reshape(dim // 2, rows), ro[layer]),
            )
        scatter[layer, which] = push(
            units.at[(layer, which) + quarter_at(a, bits[a], 1 - bits[1 - a])],
            rx1.at[layer, which], partner[1 - a],
        )

    def scatter_two(layer, which):
        scatter[layer, which].wait_recv()
        units[layer, which, :, :, y, x] = (
            units[layer, which, :, :, y, x].astype(F32) + rx1[layer, which].astype(F32)
        ).astype(BF)
        chain = Chain(
            lambda s: units.at[layer, which, s // 2, s % 2, y, x], rx2.at[layer, which]
        )
        scatter[layer, which] = chain
        chain.first()

    def scatter_three(layer, which):
        scatter[layer, which].second()

    def scatter_four(layer, which):
        scatter[layer, which].third()

    def scatter_end(layer, which):
        scatter[layer, which].end(ga_o.at[layer, which])
        store(ga_o.at[layer, which], ga_h.at[layer, which])

    def norm_forward(k, store):
        h = hbuf[...]
        centred = h - jnp.mean(h, axis=-1, keepdims=True)
        rec = lax.rsqrt(jnp.mean(centred * centred, axis=-1, keepdims=True) + EPSILON)
        normed = centred * rec
        xh[k] = normed.astype(BF)
        rstd[:, k : k + 1] = rec
        store((normed * gain[k : k + 1, :] + bias[k : k + 1, :]).astype(BF))

    def norm_backward(k, dy):
        normed = xh[k].astype(F32)
        sm[k : k + 1, :] = jnp.sum(dy * normed, axis=0, keepdims=True)
        sm[5 + k : 6 + k, :] = jnp.sum(dy, axis=0, keepdims=True)
        scaled = dy * gain[k : k + 1, :]
        first = jnp.mean(scaled, axis=-1, keepdims=True)
        second = jnp.mean(scaled * normed, axis=-1, keepdims=True)
        hbuf[...] += rstd[:, k : k + 1] * (scaled - first - normed * second)

    def into_us(k):
        def store(value):
            us[k] = value

        return store

    def into_ag(a):
        def store(value):
            ag[a, 0] = value

        return store

    def stacked(pair):
        lane = lax.broadcasted_iota(jnp.int32, pair.shape, 1)
        zero = jnp.zeros_like(pair)
        return jnp.concatenate(
            [jnp.where(lane < HEAD_DIM, pair, zero), jnp.where(lane < HEAD_DIM, zero, pair)],
            axis=0,
        )

    def merged(both_heads):
        count_rows = both_heads.shape[0] // 2
        lane = lax.broadcasted_iota(jnp.int32, (count_rows, both_heads.shape[1]), 1)
        return jnp.where(lane < HEAD_DIM, both_heads[:count_rows], both_heads[count_rows:])

    pairs = width // (2 * HEAD_DIM)

    def softmax(scores):
        top = jnp.max(scores, axis=-1, keepdims=True)
        terms = jnp.exp(scores - top)
        total = jnp.sum(terms, axis=-1, keepdims=True)
        return terms / total, top + jnp.log(total)

    def causal(scores):
        row_ids = lax.broadcasted_iota(jnp.int32, (rows, rows), 0)
        col_ids = lax.broadcasted_iota(jnp.int32, (rows, rows), 1)
        keep = col_ids <= row_ids
        return jnp.where(jnp.concatenate([keep, keep], axis=0), scores, MASKED)

    def self_forward(j):
        layer = 2 * j
        arrived((layer, "qkv"))
        u = us[layer]
        qk = dot(u, unit(layer, 0, 0, 2 * width))
        qs[j] = (qk[:, :width] + sa_b[j, 0:1, :]).astype(BF) * BF(SCALE)
        ks[j] = qk[:, width:].astype(BF)
        vs[j] = (dot(u, unit(layer, 1, 0, width)) + sa_b[j, 1:2, :]).astype(BF)
        for p in range(pairs):
            cut = slice(2 * HEAD_DIM * p, 2 * HEAD_DIM * (p + 1))
            weights, total = softmax(causal(dot_nt(stacked(qs[j, :, cut]), ks[j, :, cut])))
            lse[j, :, 2 * p : 2 * p + 1] = total[:rows]
            lse[j, :, 2 * p + 1 : 2 * p + 2] = total[rows:]
            os_[layer, :, cut] = merged(dot(weights.astype(BF), vs[j, :, cut])).astype(BF)
        arrived((layer, "out"))
        if j == 0:
            entered()
        k = exchange_start(lambda c: dot(os_[layer], wo[layer, :, pieces[c]]))
        send_attended(layer)
        return k

    def self_backward(j):
        layer = 2 * j
        low = hbuf[...].astype(BF)
        send_upstream(layer, low)
        dos[...] = dot_nt(low, wo[layer]).astype(BF)
        for p in range(pairs):
            cut = slice(2 * HEAD_DIM * p, 2 * HEAD_DIM * (p + 1))
            q2 = stacked(qs[j, :, cut])
            do2 = stacked(dos[:, cut])
            scores = causal(dot_nt(q2, ks[j, :, cut]))
            total = jnp.concatenate(
                [lse[j, :, 2 * p : 2 * p + 1], lse[j, :, 2 * p + 1 : 2 * p + 2]], axis=0
            )
            weights = jnp.exp(scores - total)
            grads = dot_nt(do2, vs[j, :, cut])
            inner = jnp.sum(weights * grads, axis=-1, keepdims=True)
            score_grad = (weights * (grads - inner)).astype(BF)
            dqk[layer, :, cut] = (SCALE * merged(dot(score_grad, ks[j, :, cut]))).astype(BF)
            dqk[layer, :, slice(width + cut.start, width + cut.stop)] = dot_tn(
                score_grad, q2
            ).astype(BF)
            dvs[j, :, cut] = dot_tn(weights.astype(BF), do2).astype(BF)
        if j == 0:
            send_grads(layer)
        k = exchange_start(
            whole(
                dot_nt(dqk[layer], unit(layer, 0, 0, 2 * width))
                + dot_nt(dvs[j], unit(layer, 1, 0, width))
            )
        )
        sm[10 + j : 11 + j, :] = column_sum(low)
        sm[16 + 2 * j : 17 + 2 * j, :width] = column_sum(dqk[layer, :, :width])
        sm[17 + 2 * j : 18 + 2 * j, :width] = column_sum(dvs[j])
        return k

    spans = rows // SPAN
    keys = nsel.shape[0] // spans

    def shift_up(values):
        moved = pltpu.roll(values, rows - (SPAN - 1), 0)
        row_ids = lax.broadcasted_iota(jnp.int32, values.shape, 0)
        return jnp.where(row_ids < rows - (SPAN - 1), moved, 0.0)

    def shift_down(values):
        moved = pltpu.roll(values, SPAN - 1, 0)
        row_ids = lax.broadcasted_iota(jnp.int32, values.shape, 0)
        return jnp.where(row_ids >= SPAN - 1, moved, 0.0)

    def cross_keys():
        arrived((1, "qkv"))
        arrived("n")
        for pick in range(pool):
            own = slice(pick * length, (pick + 1) * length)
            rows_of = pl.ds(assign[pick % 2, pick // 2] * length, length)
            nsel[own, :width] = dkn[rows_of, :]
            nsel[own, width:] = dvn[rows_of, :]
        ck[...] = dot(nsel[...], unit(1, 0, width, width)).astype(BF)
        cv[...] = (dot(nsel[...], unit(1, 1, 0, width)) + ca_b[1:2, :]).astype(BF)

    def cross_forward():
        q = dot(us[1], unit(1, 0, 0, width)) + ca_b[0:1, :]
        cq[...] = shift_up(q).astype(BF) * BF(SCALE)
        outs = []
        for c in range(spans):
            own = slice(c * SPAN, (c + 1) * SPAN)
            span_keys = slice(c * keys, (c + 1) * keys)
            parts = []
            for p in range(pairs):
                cut = slice(2 * HEAD_DIM * p, 2 * HEAD_DIM * (p + 1))
                weights, total = softmax(dot_nt(stacked(cq[own, cut]), ck[span_keys, cut]))
                lse[2, own, 2 * p : 2 * p + 1] = total[:SPAN]
                lse[2, own, 2 * p + 1 : 2 * p + 2] = total[SPAN:]
                parts.append(merged(dot(weights.astype(BF), cv[span_keys, cut])))
            outs.append(jnp.concatenate(parts, axis=1))
        os_[1] = shift_down(jnp.concatenate(outs, axis=0)).astype(BF)
        arrived((1, "out"))
        k = exchange_start(lambda c: dot(os_[1], wo[1, :, pieces[c]]))
        send_attended(1)
        return k

    def cross_backward():
        low = hbuf[...].astype(BF)
        send_upstream(1, low)
        dos[...] = shift_up(dot_nt(low, wo[1])).astype(BF)
        query_grads = []
        for c in range(spans):
            own = slice(c * SPAN, (c + 1) * SPAN)
            span_keys = slice(c * keys, (c + 1) * keys)
            parts = []
            for p in range(pairs):
                cut = slice(2 * HEAD_DIM * p, 2 * HEAD_DIM * (p + 1))
                q2 = stacked(cq[own, cut])
                do2 = stacked(dos[own, cut])
                scores = dot_nt(q2, ck[span_keys, cut])
                total = jnp.concatenate(
                    [lse[2, own, 2 * p : 2 * p + 1], lse[2, own, 2 * p + 1 : 2 * p + 2]], axis=0
                )
                weights = jnp.exp(scores - total)
                grads = dot_nt(do2, cv[span_keys, cut])
                inner = jnp.sum(weights * grads, axis=-1, keepdims=True)
                score_grad = (weights * (grads - inner)).astype(BF)
                parts.append(SCALE * merged(dot(score_grad, ck[span_keys, cut])))
                dkn[span_keys, cut] = dot_tn(score_grad, q2).astype(BF)
                dvn[span_keys, cut] = dot_tn(weights.astype(BF), do2).astype(BF)
            query_grads.append(jnp.concatenate(parts, axis=1))
        dqk[1, :, :width] = shift_down(jnp.concatenate(query_grads, axis=0)).astype(BF)
        send_grads(1)
        k = exchange_start(whole(dot_nt(dqk[1, :, :width], unit(1, 0, 0, width))))

        sm[12:13, :] = column_sum(low)
        sm[20:21, :width] = column_sum(dqk[1, :, :width])
        sm[21:22, :width] = column_sum(dvn[...])
        return k

    def neighbours_start():
        def feature_half(which):
            key_rows = units[1, 0, which, :, :, :, :, second].reshape(dim // 2, width)
            value_rows = units[1, 1, which, :, :, :, :, first].reshape(dim // 2, width)
            return dot_nt(dkn[...], key_rows) + dot_nt(dvn[...], value_rows)

        given = feature_half(1 - t).astype(BF)
        for q in range(ff // width):
            gp[1, :, q * width : (q + 1) * width] = given[q * rows : (q + 1) * rows]
        other = push(gp.at[1], gp.at[0], sib)
        nbr_sum[0] = (other, feature_half(t).astype(BF))

    def send_half(which, columns, name):
        a = axis_of(1, which)
        at = (1, which) + half_at(a, 1 - bits[a]) + (slice(None),) * a + (slice(None), columns)
        factors[name] = push(units.at[at], rx0.at[which], partner[a])

    def cross_key_weights():
        unit_store(1, 0, width, dot_tn(nsel[...], dkn[...]))
        send_half(0, second, "k")

    def cross_value_weights():
        unit_store(1, 1, 0, dot_tn(nsel[...], dvn[...]))
        send_half(1, first, "v")

    nbr_sum = [None]

    def neighbours_end():
        other, keep = nbr_sum[0]
        other.wait_recv()
        first_store = len(stores)
        taken = [gp[0, :, q * width : (q + 1) * width].astype(F32) for q in range(ff // width)]
        total = keep.astype(F32) + jnp.concatenate(taken, axis=0)
        for slot in range(pool):
            summed = jnp.zeros((length, total.shape[1]), F32)
            for pick in range(pool):
                hit = jnp.where(assign[pick % 2, pick // 2] == slot, F32(1.0), F32(0.0))
                summed += hit * total[pick * length : (pick + 1) * length]
            place = slot % nbr_o.shape[0]
            if slot >= nbr_o.shape[0]:
                stores[first_store + place].wait()
                stores[first_store + place] = None
            nbr_o[place] = summed
            store(nbr_o.at[place], nbr_h.at[slot])

    cuts = [slice(c * dim, (c + 1) * dim) for c in range(ff // dim)]

    def mlp_forward(j):
        if j == 0:
            arrived("mlp0")
        part = None
        for cut in cuts[:-1]:
            pre = dot(ag[2 * j, 0], win[j, :, cut]) + in_b[j : j + 1, cut]
            active, slope = gelu_parts(pre)
            gp[j, :, cut] = slope.astype(BF)
            term = dot(active.astype(BF), wout[j, cut, :])
            part = term if part is None else part + term
        cut = cuts[-1]
        pre = dot(ag[2 * j, 0], win[j, :, cut]) + in_b[j : j + 1, cut]
        active, slope = gelu_parts(pre)
        gp[j, :, cut] = slope.astype(BF)
        active = active.astype(BF)
        return exchange_start(lambda c: whole(part)(c) + dot(active, wout[j, cut, pieces[c]]))

    def down_early():
        for q in range(ff // width):
            cut = slice(q * width, (q + 1) * width)
            dkn[q * rows : (q + 1) * rows, :] = dot_nt(ag[3, 0], wout[1, cut, :]).astype(BF)

    def mlp_backward(j, before=None):
        low = ag[2 * j + 1, 0]
        sm[13 + j : 14 + j, :] = column_sum(low)
        grads = []
        for c, cut in enumerate(cuts):
            if j == 1:
                per = dim // width
                down = jnp.concatenate(
                    [
                        dkn[q * rows : (q + 1) * rows, :].astype(F32)
                        for q in range(c * per, (c + 1) * per)
                    ],
                    axis=1,
                )
            else:
                down = dot_nt(low, wout[j, cut, :])
            pre_grad = (down * gp[j, :, cut].astype(F32)).astype(BF)
            grads.append(pre_grad)
        part = None
        for pre_grad, cut in zip(grads[:-1], cuts[:-1]):
            term = dot_nt(pre_grad, win[j, :, cut])
            part = term if part is None else part + term
        if before is not None:
            before()
        k = exchange_start(
            lambda c: whole(part)(c) + dot_nt(grads[-1], win[j, pieces[c], cuts[-1]])
        )
        for c, pre_grad in enumerate(grads):
            sm[24 + 2 * j + c : 25 + 2 * j + c, :] = column_sum(pre_grad)
        return k

    def mlp_rows(j):
        gather_wait(2 * j)
        gather_wait(2 * j + 1)

        def bucket(b, carry):
            for c in range(2):
                turn(turned, ag[2 * j + c, b])
                part = turned[:, :, y, x] if j == 0 else turned[z1, z0]
                turned_rows[c, b] = part.reshape(4 * block, rows)
            return carry

        lax.fori_loop(0, 4, bucket, 0)

    def mlp_weights(j, c):
        cut = cuts[c]
        acc[...] = jnp.zeros_like(acc)

        def bucket(b, carry):
            pre = dot(ag[2 * j, b], win[j, :, cut]) + in_b[j : j + 1, cut]
            active, slope = gelu_parts(pre)
            pre_grad = (dot_nt(ag[2 * j + 1, b], wout[j, cut, :]) * slope).astype(BF)
            acc[0] += dot(turned_rows[0, b], pre_grad)
            acc[1] += dot(turned_rows[1, b], active.astype(BF))
            return carry

        lax.fori_loop(0, 4, bucket, 0, unroll=2)
        zst[j, c] = acc[...].astype(BF).reshape(2, 2, 2, block, dim)
        if j == 0:
            chain = Chain(lambda s: zst.at[0, c, :, s // 2, s % 2], rz.at[c])
            scatter["z", c] = chain
            chain.first()
        elif c == 0:
            scatter["w", c] = push(zst.at[1, c, :, :, 1 - x], rw0.at[c], px)
        else:
            scatter["w", c] = push(zst.at[1, c, :, 1 - y], rw0.at[c], py)

    def mlp_second(c):
        scatter["w", c].wait_recv()
        got = rw0[c].astype(F32)
        if c == 0:
            zst[1, c, :, :, x] = (zst[1, c, :, :, x].astype(F32) + got).astype(BF)
            scatter["w", c] = push(zst.at[1, c, :, 1 - y, x], rw1.at[c], py)
        else:
            zst[1, c, :, y] = (zst[1, c, :, y].astype(F32) + got).astype(BF)
            scatter["w", c] = push(zst.at[1, c, :, y, 1 - x], rw1.at[c], px)

    def mlp_end(j, c):
        if j == 0:
            scatter["z", c].end(gm_o.at[j, c])
        else:
            scatter["w", c].wait_recv()
            gm_o[j, c] = zst[1, c, :, y, x].astype(F32) + rw1[c].astype(F32)
        store(gm_o.at[j, c], gm_h.at[j, :, :, pl.ds(c * dim, dim)])

    live = lax.broadcasted_iota(jnp.int32, (rows, dim), 0) < lengths[0]
    sm[...] = jnp.zeros_like(sm)
    hbuf[...] = hidden[...].astype(F32)
    norm_forward(0, into_us(0))
    k = self_forward(0)
    send_inputs(0)
    arrived("cot")
    ag[3, 0] = jnp.where(live, ag[3, 0], jnp.zeros((rows, dim), BF))
    gather_start(3, (pz0, pz1, pz))
    cross_keys()
    hbuf[...] += exchange_wait(k) + sa_ob[0:1, :]
    norm_forward(1, into_us(1))
    k = cross_forward()
    send_inputs(1)
    hbuf[...] += exchange_wait(k) + ca_ob[...].reshape(1, dim)
    norm_forward(2, into_ag(0))
    gather_start(0)
    k = mlp_forward(0)
    arrived("mlp1")
    down_early()
    hbuf[...] += exchange_wait(k) + out_b[0:1, :]
    norm_forward(3, into_us(2))
    k = self_forward(1)
    send_inputs(2)
    hbuf[...] += exchange_wait(k) + sa_ob[1:2, :]
    norm_forward(4, into_ag(2))
    gather_start(2, (pz0, pz1, pz))
    last = mlp_forward(1)
    gather_forward(0)

    small_copy = []
    small_bufs = [sm] + [small_o.at[q] for q in range(4)]

    def small_step(k):
        if k:
            small_copy[-1].wait_recv()
            small_bufs[k][...] = small_bufs[k - 1][...] + rsm[k - 1]
        if k < 4:
            small_copy.append(push(small_bufs[k], rsm.at[k], (px, py, pz0, pz1)[k]))
            return
        small = small_o.at[3]
        gain_o[...] = small[0:5, :]
        bias_o[...] = small[5:10, :]
        sa_ob_o[...] = small[10:12, :]
        ca_ob_o[...] = small[12, :]
        out_b_o[...] = small[13:15, :]
        for j in range(2):
            sa_b_o[j] = small[16 + 2 * j : 18 + 2 * j, :width]
            for c, cut in enumerate(cuts):
                in_b_o[j : j + 1, cut] = small[24 + 2 * j + c : 25 + 2 * j + c, :]
        ca_b_o[...] = small[20:22, :width]
        for src, dst in (
            (gain_o, gain_h), (bias_o, bias_h), (sa_ob_o, sa_ob_h), (ca_ob_o, ca_ob_h),
            (out_b_o, out_b_h), (sa_b_o, sa_b_h), (ca_b_o, ca_b_h), (in_b_o, in_b_h),
        ):
            store(src, dst)

    pending = {}

    def begin(norm, call, *args):
        pending[norm] = call(*args)

    def finish_norm(norm):
        norm_backward(norm, exchange_wait(pending[norm]))

    def first_grads():
        ag[1, 0] = hbuf[...].astype(BF)
        gather_start(1, (px, py, pxy))

    def last_norm():
        finish_norm(0)
        store(hbuf, grad_h)

    def feed_forward_back():
        def output():
            final = hbuf[...] + exchange_wait(last) + out_b[1:2, :]
            hid_o[...] = jnp.where(live, final, 0.0).astype(BF)
            store(hid_o, hid_h)
            hbuf[...] = ag[3, 0].astype(F32)

        begin(4, mlp_backward, 1, output)
        finish_norm(4)

    steps = {
        "b1": feed_forward_back,
        "b0a": partial(begin, 2, mlp_backward, 0),
        "b0b": partial(finish_norm, 2),
        "S2a": partial(begin, 3, self_backward, 1),
        "S2b": partial(finish_norm, 3),
        "S0a": partial(begin, 0, self_backward, 0),
        "S0b": last_norm,
        "d1": first_grads,
        "g2": lambda: send_grads(2),
        "Ca": partial(begin, 1, cross_backward),
        "Cb": partial(finish_norm, 1),
        "Cn": neighbours_start,
        "Ck": cross_key_weights,
        "Cv": cross_value_weights,
        "gswd2": lambda: gather_swap(3),
        "gswd1": lambda: gather_swap(1),
        "gswu2": lambda: gather_swap(2),
        "gru1": lambda: gather_relay(0),
        "rows0": lambda: mlp_rows(0),
        "rows1": lambda: mlp_rows(1),
        "nbr": neighbours_end,
    }
    for n in range(5):
        steps["sm%d" % n] = partial(small_step, n)
    for n in range(2):
        steps["mw0%d" % n] = partial(mlp_weights, 0, n)
        steps["mw1%d" % n] = partial(mlp_weights, 1, n)
        steps["mz2%d" % n] = lambda n=n: scatter["z", n].second()
        steps["mz3%d" % n] = lambda n=n: scatter["z", n].third()
        steps["mze%d" % n] = partial(mlp_end, 0, n)
        steps["ms%d" % n] = partial(mlp_second, n)
        steps["me%d" % n] = partial(mlp_end, 1, n)
    for layer in range(3):
        steps["rf%d" % layer] = partial(relay_factors, layer)
        for n in range(2):
            steps["s1%s%d" % ("ab"[n], layer)] = partial(scatter_one, layer, n)
            steps["s2%d%d" % (layer, n)] = partial(scatter_two, layer, n)
            steps["s3%d%d" % (layer, n)] = partial(scatter_three, layer, n)
            steps["s4%d%d" % (layer, n)] = partial(scatter_four, layer, n)
            steps["se%d%d" % (layer, n)] = partial(scatter_end, layer, n)
    for name in ORDER:
        steps[name]()
    for copy in stores:
        if copy is not None:
            copy.wait()
    for copy in sends:
        copy.wait_send()
    for chain in chains:
        chain.sent()
    for k in (ex[0] - 2, ex[0] - 1):
        for copy in ex_copy[k]:
            copy.wait_send()


def finish(*refs):
    parts, outs = refs[:13], refs[13:30]
    held, get, put = refs[30:43], refs[43], refs[44]
    (
        hid_o, grad_o, nbr_o, gain_o, bias_o, sa_qkv_o, sa_b_o, sa_out_o, sa_ob_o, ca_qkv_o,
        ca_b_o, ca_out_o, ca_ob_o, in_o, in_b_o, out_o, out_b_o,
    ) = outs
    width = ca_out_o.shape[1]
    ga, gm = held[3], held[4]
    places = {
        0: [(held[0], hid_o)],
        1: [(held[1], grad_o)],
        2: [(held[2], nbr_o)],
        3: [],
        4: [(gm.at[j, c], out.at[j]) for j in range(2) for c, out in enumerate((in_o, out_o))],
    }
    for a, out, rows in (
        (0, sa_qkv_o.at[0], sa_out_o.at[0]), (1, ca_qkv_o, ca_out_o),
        (2, sa_qkv_o.at[1], sa_out_o.at[1]),
    ):
        for c in range(4):
            src = ga.at[a, c // 2, :, pl.ds(c % 2 * width, width)]
            places[3].append((src, rows if c == 3 else out.at[c]))
    for k, out in enumerate((gain_o, bias_o, sa_ob_o, ca_ob_o, out_b_o, sa_b_o, ca_b_o, in_b_o)):
        places[5 + k] = [(held[5 + k], out)]
    order = (2, 4, 3, 1, 0) + tuple(range(5, 13))
    fetched = {}
    for k in order:
        fetched[k] = pltpu.make_async_copy(parts[k], held[k], get.at[k])
        fetched[k].start()
    copies = []
    for k in order:
        fetched[k].wait()
        for src, dst in places[k]:
            copies.append(pltpu.make_async_copy(src, dst, put.at[len(copies)]))
            copies[-1].start()
    for copy in copies:
        copy.wait()


def on_device(
    n_dp,
    hidden_in, lengths, neighbours, assign, cotangent, norm_gain, norm_bias, sa_qkv, sa_bias,
    sa_out, sa_out_bias, ca_qkv, ca_bias, ca_out, ca_out_bias, mlp_in, mlp_in_bias, mlp_out,
    mlp_out_bias,
):
    rows, dim = hidden_in.shape
    width = sa_out.shape[1]
    ff = mlp_in.shape[2]
    pool, length = neighbours.shape[0], neighbours.shape[1]
    block = dim // GROUPS
    picks = assign.size * length
    vmem = pl.BlockSpec(memory_space=pltpu.VMEM)
    smem = pl.BlockSpec(memory_space=pltpu.SMEM)
    hbm = pl.BlockSpec(memory_space=pl.ANY)

    def array(*shape, dtype=F32):
        return jax.ShapeDtypeStruct(shape, dtype)

    outs = (
        array(rows, dim, dtype=BF),
        array(rows, dim),
        array(pool, length, width),
        array(3, 2, block, 2 * width),
        array(2, 2, block, ff),
        array(5, dim),
        array(5, dim),
        array(2, dim),
        array(dim),
        array(2, dim),
        array(2, 2, width),
        array(2, width),
        array(2, ff),
    )
    V = pltpu.VMEM
    scratch = [
        V((rows, dim), BF),
        V((pool // 2, length, width), F32),
        V((3, 2, block, 2 * width), F32),
        V((2, ff // dim, 2, block, dim), F32),
        V((4, SMALL_ROWS, dim), F32),
    ] + [V(out.shape, F32) for out in outs[5:]] + [
        V((3, 2, 2, 2, 2, 2, block, 2 * width), BF),
        V((3, width, dim), BF),
        V((2, dim, ff), BF),
        V((2, ff, dim), BF),
        V((picks, dim), BF),
        V((4, 4, rows, dim), BF),
        V((3, rows, dim), BF),
        V((5, rows, dim), BF),
        V((rows, 128), F32),
        V((2, rows, width), BF),
        V((2, rows, width), BF),
        V((2, rows, width), BF),
        V((3, rows, width), BF),
        V((rows, width), BF),
        V((picks, width), BF),
        V((picks, width), BF),
        V((3, rows, 128), F32),
        V((2, rows, ff), BF),
        V((3, rows, 2 * width), BF),
        V((2, rows, width), BF),
        V((picks, width), BF),
        V((picks, width), BF),
        V((rows, width), BF),
        V((2, rows, dim), BF),
        V((2, rows, dim), BF),
        V((2, 2, 2, 2, block, width), BF),
        V((3, 2, 2, 2, block, 2 * width), BF),
        V((3, 2, 5, block, 2 * width), BF),
        V((2, 4 * block, dim), F32),
        V((2, ff // dim, 2, 2, 2, block, dim), BF),
        V((ff // dim, 5, 2, block, dim), BF),
        V((ff // dim, 2, 2, block, dim), BF),
        V((ff // dim, 2, block, dim), BF),
        V((SMALL_ROWS, dim), F32),
        V((4, SMALL_ROWS, dim), F32),
        V((rows, dim), F32),
        V((3, 2, 2, 2, 2, block, rows), BF),
        V((3, 2, 2, 2, 2, block, rows), BF),
        V((3, 2, 2, 2, block, rows), BF),
        V((2, 2, 2, 2, block, rows), BF),
        V((3, 2, 2, 2, block, rows), BF),
        V((3, rows, width), BF),
        V((3, rows, 2 * width), BF),
        V((2, rows, width), BF),
        V((2, 2, 2, 2, block, rows), BF),
        V((2, 4, 4 * block, rows), BF),
        pltpu.SemaphoreType.DMA((64,)),
        pltpu.SemaphoreType.DMA((160,)),
        pltpu.SemaphoreType.DMA((160,)),
    ]
    hid, grad, nbr, ga, gm, *small = pl.pallas_call(
        partial(kernel, n_dp),
        out_shape=outs,
        in_specs=[smem] * 2 + [vmem] * 9 + [hbm] * 8,
        out_specs=(hbm,) * 13,
        scratch_shapes=scratch,
        compiler_params=pltpu.CompilerParams(
            collective_id=0, has_side_effects=True, vmem_limit_bytes=64 * 1024 * 1024 - 65536
        ),
    )(
        lengths, assign.T, norm_gain, norm_bias, sa_bias, sa_out_bias,
        ca_bias, ca_out_bias, mlp_in_bias, mlp_out_bias,
        hidden_in, cotangent, neighbours, sa_qkv, sa_out, ca_qkv, ca_out, mlp_in, mlp_out,
    )
    rest = n_dp // GROUPS
    if rest > 1:
        members = [[a * rest + b for b in range(rest)] for a in range(GROUPS)]
        ga = lax.psum_scatter(ga, "dp", scatter_dimension=2, axis_index_groups=members, tiled=True)
        gm = lax.psum_scatter(gm, "dp", scatter_dimension=2, axis_index_groups=members, tiled=True)
        small = lax.psum(small, "dp", axis_index_groups=members)
    owned = block // rest
    results = pl.pallas_call(
        finish,
        out_shape=(
            outs[0],
            outs[1],
            outs[2],
            array(5, dim),
            array(5, dim),
            array(2, 3, owned, width),
            array(2, 2, width),
            array(2, owned, width),
            array(2, dim),
            array(3, owned, width),
            array(2, width),
            array(owned, width),
            array(dim),
            array(2, owned, ff),
            array(2, ff),
            array(2, owned, ff),
            array(2, dim),
        ),
        in_specs=[hbm] * 13,
        out_specs=(hbm,) * 17,
        scratch_shapes=[
            V((rows, dim), BF),
            V((rows, dim), F32),
            V((pool, length, width), F32),
            V((3, 2, owned, 2 * width), F32),
            V((2, 2, owned, ff), F32),
        ]
        + [V(out.shape, F32) for out in outs[5:]]
        + [pltpu.SemaphoreType.DMA((16,)), pltpu.SemaphoreType.DMA((32,))],
    )(hid, grad, nbr, ga, gm, *small)
    results = list(results)
    for k in (7, 11, 15):
        results[k] = results[k].swapaxes(-1, -2)
    return tuple(results)


def solution(mesh):
    return jax.shard_map(
        partial(on_device, mesh.shape["dp"]),
        mesh=mesh,
        in_specs=(
            P("dp", None),
            P("dp"),
            P("dp", None, None),
            P("dp", None),
            P("dp", None),
            P(),
            P(),
            P(None, None, None, "tensor"),
            P(None, None, "tensor"),
            P(None, "tensor", None),
            P(),
            P(None, None, "tensor"),
            P(None, "tensor"),
            P("tensor", None),
            P(),
            P(None, None, "tensor"),
            P(None, "tensor"),
            P(None, "tensor", None),
            P(),
        ),
        out_specs=(
            P("dp", None),
            P("dp", None),
            P("dp", None, "tensor"),
            P(),
            P(),
            P(None, None, "dp", "tensor"),
            P(None, None, "tensor"),
            P(None, "tensor", "dp"),
            P(),
            P(None, "dp", "tensor"),
            P(None, "tensor"),
            P("tensor", "dp"),
            P(),
            P(None, "dp", "tensor"),
            P(None, "tensor"),
            P(None, "tensor", "dp"),
            P(),
        ),
        check_vma=False,
    )
```
